32 devices in a mesh: win: 2 (over y), row: 4 (over z), col: 4 (over x, core).
Axes of the slice: x: 2, y: 2, z: 4, core: 2. Of those that a mesh axis runs over, the one named last changes fastest.
Arguments:
- records: bfloat16 [32, 4096, 1024], P('win', ('row', 'col'))
- tile_pairs: int32 [4, 4, 4, 2], P('row', 'col'), may hold values from 0 to 3
- tile_count: int32 [4, 4], P('row', 'col'), may hold values from 1 to 4, as said below
- bin_index: int32 [32], replicated, may hold values from 1 to 511, as said below
Outputs:
- cross_tiles: bfloat16 [4, 4, 4, 2, 32, 256, 256], P('row', 'col', 'win')
The draws below stay inside these ranges and needn't reach their ends.
Inputs may be any that keep to these rules, and one draw needn't show every extreme that they name: Slots 0 to tile_count - 1 of a cell are live; some cell has all 4 live and some cell one. `bin_index`: distinct and increasing; the first is 1 and the last 511.
All inputs are finite; a program needn't handle non-finite values.
Results may differ from the reference program's by a relative error of at most 0.0069.
Values may be sent and summed in bfloat16 or wider, within the bound.
A program may use at most 256 MiB of HBM per device.

```python
import math
import jax
import jax.numpy as jnp
from jax import lax

CHAN_BLOCK = 256
SAMPLES = 1024
KEPT_BINS = 32
SLOTS = 4
GRID_SIDE = 4
WINDOWS = 32
CHANNELS = 4096


def draw_records(key, part):
    keys = jax.random.split(key, 3)
    noise = jax.random.normal(keys[0], (WINDOWS, CHANNELS, SAMPLES), jnp.float32)
    spread = math.log(10.0)
    window_scale = jnp.exp(jax.random.uniform(keys[1], (WINDOWS, 1, 1), jnp.float32, 0.0, spread))
    channel_scale = jnp.exp(jax.random.uniform(keys[2], (1, CHANNELS, 1), jnp.float32, 0.0, spread))
    return (noise * window_scale * channel_scale).astype(jnp.bfloat16)


def draw_tile_count(key, part):
    keys = jax.random.split(key, 3)
    cells = GRID_SIDE * GRID_SIDE
    counts = jax.random.randint(keys[0], (cells,), 1, SLOTS + 1, dtype=jnp.int32)
    highest = jax.random.randint(keys[1], (), 0, cells, dtype=jnp.int32)
    lowest = (highest + 1 + jax.random.randint(keys[2], (), 0, cells - 1, dtype=jnp.int32)) % cells
    counts = counts.at[highest].set(SLOTS)
    counts = counts.at[lowest].set(1)
    return counts.reshape(GRID_SIDE, GRID_SIDE).astype(jnp.int32)


def draw_bin_index(key, part):
    inner = jax.random.permutation(key, SAMPLES // 2 - 3)[:KEPT_BINS - 2].astype(jnp.int32) + 2
    inner = jnp.sort(inner)
    first = jnp.ones((1,), jnp.int32)
    final = jnp.full((1,), SAMPLES // 2 - 1, jnp.int32)
    return jnp.concatenate([first, inner, final]).astype(jnp.int32)


def plant(result, rng, smallest, top_value):
    shape = result.shape
    place = [jax.random.randint(jax.random.fold_in(rng, axis), (), 0, shape[axis]) for axis in range(len(shape))]
    result = result.at[tuple(place)].set(smallest)
    longest = shape.index(max(shape))
    place[longest] = (place[longest] + 1) % shape[longest]
    return result.at[tuple(place)].set(top_value)


def setup_inputs(seed: int = 0) -> dict:
    key_list = jax.random.split(jax.random.key(seed), 5)
    records = draw_records(jax.random.fold_in(key_list[4], 71), 0)
    tile_pairs = plant(jax.random.randint(key_list[1], (GRID_SIDE, GRID_SIDE, SLOTS, 2), 0, GRID_SIDE), jax.random.fold_in(key_list[1], 1), 0, GRID_SIDE - 1).astype(jnp.int32)
    tile_count = draw_tile_count(jax.random.fold_in(key_list[4], 71), 0)
    bin_index = draw_bin_index(jax.random.fold_in(key_list[4], 71), 0)
    return {"records": records, "tile_pairs": tile_pairs, "tile_count": tile_count, "bin_index": bin_index}


def dft_table(bin_index, length):
    sample_ids = jnp.arange(length, dtype=jnp.int32)
    phases = sample_ids[:, None] * bin_index[None, :] % length
    angles = 2.0 * math.pi / length * phases.astype(jnp.float32)
    window_taper = 0.5 - 0.5 * jnp.cos(2.0 * math.pi / length * sample_ids.astype(jnp.float32))
    cosine = window_taper[:, None] * jnp.cos(angles)
    sine = -window_taper[:, None] * jnp.sin(angles)
    return jnp.concatenate([cosine, sine], axis=1).astype(jnp.bfloat16)

def reference(records, tile_pairs, tile_count, bin_index):
    phase_table = dft_table(bin_index, SAMPLES)

    def whiten_window(window_rows):
        spectrum = jnp.dot(window_rows, phase_table, preferred_element_type=jnp.float32)
        energy = jnp.sqrt(lax.optimization_barrier(jnp.mean(spectrum * spectrum, axis=1, keepdims=True)) + 1e-06)
        return (spectrum / energy).astype(jnp.bfloat16)
    whitened = lax.map(whiten_window, records)
    blocks = whitened.reshape(WINDOWS, GRID_SIDE * GRID_SIDE, CHAN_BLOCK, 2, KEPT_BINS)
    flat_pairs = tile_pairs.reshape(GRID_SIDE * GRID_SIDE * SLOTS, 2).astype(jnp.int32)
    flat_count = tile_count.reshape(GRID_SIDE * GRID_SIDE).astype(jnp.int32)
    item_ids = jnp.arange(GRID_SIDE * GRID_SIDE * SLOTS, dtype=jnp.int32)

    def one_tile(item):
        cell = item // SLOTS
        slot = item % SLOTS
        grid_row = cell // GRID_SIDE
        grid_col = cell % GRID_SIDE
        first_id = grid_row * GRID_SIDE + flat_pairs[item, 0]
        second_id = flat_pairs[item, 1] * GRID_SIDE + grid_col
        first_block = blocks[:, first_id].astype(jnp.float32)
        second_block = blocks[:, second_id].astype(jnp.float32)
        first_real = first_block[:, :, 0]
        first_imag = first_block[:, :, 1]
        second_real = second_block[:, :, 0]
        second_imag = second_block[:, :, 1]
        real_part = jnp.einsum('wpk,wqk->kpq', first_real, second_real) + jnp.einsum('wpk,wqk->kpq', first_imag, second_imag)
        imag_part = jnp.einsum('wpk,wqk->kpq', first_imag, second_real) - jnp.einsum('wpk,wqk->kpq', first_real, second_imag)
        live = (slot < flat_count[cell]).astype(jnp.float32)
        return (jnp.stack([real_part, imag_part]) * live).astype(jnp.bfloat16)
    tiles = lax.map(one_tile, item_ids)
    return tiles.reshape(GRID_SIDE, GRID_SIDE, SLOTS, 2, KEPT_BINS, CHAN_BLOCK, CHAN_BLOCK)
```

```python
import functools
import math

import jax
import jax.numpy as jnp
from jax import lax
from jax.experimental import pallas as pl
from jax.experimental.pallas import tpu as pltpu
from jax.sharding import PartitionSpec as P

GROUP = 8
FETCH = 4
UP, DOWN, PARTNER, RIGHT, LEFT, SIBLING = range(6)


def chunk_list(bins):
    size = max(bins // 8, 1)
    return [(k, min(size, bins - k)) for k in range(0, bins, size)]


def cos_sin(phase, length):
    quarter = length // 4
    turn = (phase + quarter // 2) // quarter
    x = (phase - turn * quarter).astype(jnp.float32) * (2.0 * math.pi / length)
    y = x * x
    c = 1.0 + y * (-0.5 + y * (1.0 / 24 + y * (-1.0 / 720 + y * (1.0 / 40320))))
    s = x * (1.0 + y * (-1.0 / 6 + y * (1.0 / 120 + y * (-1.0 / 5040 + y * (1.0 / 362880)))))
    odd = turn % 2 == 1
    cosine, sine = jnp.where(odd, s, c), jnp.where(odd, c, s)
    turn = turn % 4
    cosine = jnp.where((turn == 1) | (turn == 2), -cosine, cosine)
    sine = jnp.where(turn >= 2, -sine, sine)
    return cosine, sine


def fill_table(bin_ref, kcol, table, length):
    bins = kcol.shape[0]
    for k in range(bins):
        kcol[k:k + 1, :] = jnp.full((1, 128), bin_ref[k], jnp.int32)
    for lane in range(0, length, 128):
        samples = lax.broadcasted_iota(jnp.int32, (8, 128), 1) + lane
        taper = 0.5 - 0.5 * cos_sin(samples, length)[0]
        taper = jnp.concatenate([taper] * (bins // 8), axis=0)
        samples = jnp.concatenate([samples] * (bins // 8), axis=0)
        cosine, sine = cos_sin(kcol[...] * samples % length, length)
        table[:bins, lane:lane + 128] = (taper * cosine).astype(jnp.bfloat16)
        table[bins:, lane:lane + 128] = (-taper * sine).astype(jnp.bfloat16)


def gather_kernel(rows, cols, chunks, pairs, bin_ref, rec_hbm, row_set, col_pick,
                  kcol, table, rec, spec, own, stage, *rest):
    col = rest[:len(chunks)]
    (rec_sem, local_sem, row_send, row_recv, hop_send, hop_recv, pick_send, pick_recv,
     pick_local) = rest[len(chunks):]
    groups, bins = own.shape[0], own.shape[1]
    owned = stage.shape[1]
    w, r, q = lax.axis_index("win"), lax.axis_index("row"), lax.axis_index("col")
    chips = cols // 2
    x = q // 2
    other = 1 - w
    device = {
        UP: (w, r + 1, q), DOWN: (w, r - 1, q), PARTNER: (other, r, q),
        RIGHT: (w, r, q + 2), LEFT: (w, r, q - 2), SIBLING: (w, r, q + 1 - 2 * (q % 2)),
    }
    exists = {
        UP: r < rows - 1, DOWN: r > 0, PARTNER: None,
        RIGHT: x < chips - 1, LEFT: x > 0, SIBLING: None,
    }

    def fetch(i):
        part = pl.ds(i * FETCH, FETCH)
        return pltpu.make_async_copy(rec_hbm.at[part], rec.at[part], rec_sem.at[i])

    for i in range(groups * GROUP // FETCH):
        fetch(i).start()

    def guarded(way, f):
        if exists[way] is None:
            f()
        else:
            pl.when(exists[way])(f)

    barrier = pltpu.get_barrier_semaphore()
    for way in range(6):
        guarded(way, lambda way=way: pl.semaphore_signal(
            barrier, inc=1, device_id=device[way], device_id_type=pl.DeviceIdType.MESH))
    ends = sum(exists[way].astype(jnp.int32) for way in (UP, DOWN, RIGHT, LEFT))

    pending = []

    def send(way, make, cond=None):
        def go():
            guarded(way, lambda: make().start())

        def done():
            guarded(way, lambda: make().wait_send())

        if cond is None:
            go()
        pending.append((cond, done))
        return go

    def remote(way, src, dst, send_sem, recv_sem):
        return pltpu.make_async_remote_copy(
            src_ref=src, dst_ref=dst, send_sem=send_sem, recv_sem=recv_sem,
            device_id=device[way], device_id_type=pl.DeviceIdType.MESH)

    def row_copy(way, src, slot, part):
        return remote(way, src, row_set.at[slot, part],
                      row_send.at[way, slot, part], row_recv.at[slot, part])

    def row_arrived(slot, part):
        row_copy(PARTNER, row_set.at[slot, part], slot, part).wait_recv()

    def row_relay(cond, slot, part, ways):
        goes = [send(way, lambda way=way: row_copy(way, row_set.at[slot, part], slot, part), cond)
                for way in ways]

        def go():
            row_arrived(slot, part)
            for f in goes:
                f()

        pl.when(cond)(go)

    def along_x(part):
        for d in range(1, chips):
            row_relay(x - d >= 0, q - 2 * d, part, (RIGHT, SIBLING))
            row_relay(x + d < chips, q + 2 * d, part, (LEFT, SIBLING))

    def from_partner(g):
        part = groups + g
        row_arrived(q, part)
        for way in (RIGHT, LEFT, SIBLING):
            send(way, lambda way=way: row_copy(way, row_set.at[q, part], q, part))

    def own_hop(way, c, g):
        k, n = chunks[c]
        return remote(way, own.at[g, pl.ds(k, n)], col[c].at[r, g],
                      hop_send.at[way, r, c, g], hop_recv.at[r, c, g])

    def later_hop(way, slot, c):
        return remote(way, col[c].at[slot], col[c].at[slot],
                      hop_send.at[way, slot, c, 0], hop_recv.at[slot, c, 0])

    def hop(h, c):
        for cond, slot, way in ((r - h >= 0, r - h, UP), (r + h < rows, r + h, DOWN)):
            go_on = send(way, lambda slot=slot, way=way: later_hop(way, slot, c), cond)

            def go(slot=slot, go_on=go_on):
                if h == 1:
                    for g in range(groups):
                        remote(PARTNER, own.at[g, pl.ds(*chunks[c])], col[c].at[slot, g],
                               hop_send.at[0, slot, c, g], hop_recv.at[slot, c, g]).wait_recv()
                else:
                    later_hop(PARTNER, slot, c).wait_recv()
                go_on()

            pl.when(cond)(go)

    def pick_copy(c):
        k, n = chunks[c]
        return remote(PARTNER, stage.at[1, :, :, pl.ds(k, n)],
                      col_pick.at[:, pl.ds(groups, groups), pl.ds(k, n)],
                      pick_send.at[c], pick_recv.at[c])

    def pick_keep(c):
        k, n = chunks[c]
        return pltpu.make_async_copy(
            stage.at[0, :, :, pl.ds(k, n)],
            col_pick.at[:, pl.ds(0, groups), pl.ds(k, n)], pick_local.at[c])

    def pick(c):
        k, n = chunks[c]
        for side, half in ((1, other), (0, w)):
            for t in range(owned):
                j = pairs[0, 0, 1, half * owned + t]
                stage[side, t, :, k:k + n] = col[c][j]
            if side:
                send(PARTNER, lambda: pick_copy(c))
            else:
                pick_keep(c).start()

    fill_table(bin_ref, kcol, table, rec.shape[2])
    keeps = []
    for g in range(groups):
        for i in range(g * GROUP // FETCH, (g + 1) * GROUP // FETCH):
            fetch(i).wait()
            for v in range(i * FETCH, (i + 1) * FETCH):
                s = lax.dot_general(table[...], rec[v], (((1,), (1,)), ((), ())),
                                    preferred_element_type=jnp.float32)
                scale = 1.0 / jnp.sqrt(jnp.mean(s * s, axis=0, keepdims=True) + 1e-06)
                s = s * scale
                first = v % GROUP
                for lane in range(spec.shape[0]):
                    part = s[:, lane * 128:(lane + 1) * 128]
                    spec[lane, pl.ds(first, bins, stride=2 * GROUP), :] = part[:bins]
                    spec[lane, pl.ds(first + GROUP, bins, stride=2 * GROUP), :] = part[bins:]
        for lane in range(spec.shape[0]):
            part = spec[lane].astype(jnp.bfloat16).reshape(bins, 2 * GROUP, 128)
            own[g, :, :, lane * 128:(lane + 1) * 128] = part
            for c, (k, n) in enumerate(chunks):
                col[c][r, g, :, :, lane * 128:(lane + 1) * 128] = part[k:k + n]
        if g == 0:
            pl.semaphore_wait(barrier, 2 + ends)
        for c in range(len(chunks)):
            for way in (UP, DOWN):
                send(way, lambda way=way, c=c, g=g: own_hop(way, c, g))
            if c == 0:
                send(PARTNER, lambda g=g: remote(
                    PARTNER, own.at[g], row_set.at[q, groups + g],
                    row_send.at[PARTNER, q, groups + g], row_recv.at[q, groups + g]))
                for way in (RIGHT, LEFT, SIBLING):
                    send(way, lambda way=way, g=g: row_copy(way, own.at[g], q, g))
        keep = pltpu.make_async_copy(own.at[g], row_set.at[q, g], local_sem.at[g])
        keep.start()
        keeps.append(keep)

    last = len(chunks) + rows - 2
    for step in range(last):
        for h in range(1, rows):
            if 0 <= step - h + 1 < len(chunks):
                hop(h, step - h + 1)
        done = step - rows + 2
        if done >= 0:
            pick(done)
        if done == 1:
            for g in range(groups):
                from_partner(g)
                along_x(g)
        if done == len(chunks) // 2 + 1:
            for g in range(groups):
                along_x(groups + g)

    for c in range(chips):
        for part in range(2 * groups):
            row_arrived(2 * c + 1 - q % 2, part)
    for c in range(len(chunks)):
        pick_copy(c).wait_recv()
        pick_keep(c).wait()
    for keep in keeps:
        keep.wait()
    for cond, done in pending:
        if cond is None:
            done()
        else:
            pl.when(cond)(done)


def gather(records, pairs, bin_index, rows, cols, owned):
    windows, channels, length = records.shape
    groups = windows // GROUP
    bins = bin_index.shape[0]
    chunks = chunk_list(bins)
    count = len(chunks)
    smem = pl.BlockSpec(memory_space=pltpu.SMEM)
    hbm = pl.BlockSpec(memory_space=pl.ANY)
    dma = pltpu.SemaphoreType.DMA
    tile = (2 * GROUP, channels)
    return pl.pallas_call(
        functools.partial(gather_kernel, rows, cols, chunks),
        out_shape=(
            jax.ShapeDtypeStruct((cols, 2 * groups, bins) + tile, jnp.bfloat16),
            jax.ShapeDtypeStruct((owned, 2 * groups, bins) + tile, jnp.bfloat16)),
        in_specs=[smem, smem, hbm],
        out_specs=(hbm, hbm),
        scratch_shapes=[
            pltpu.VMEM((bins, 128), jnp.int32),
            pltpu.VMEM((2 * bins, length), jnp.bfloat16),
            pltpu.VMEM(records.shape, jnp.bfloat16),
            pltpu.VMEM((channels // 128, 2 * bins * GROUP, 128), jnp.float32),
            pltpu.VMEM((groups, bins) + tile, jnp.bfloat16),
            pltpu.VMEM((2, owned, groups, bins) + tile, jnp.bfloat16),
            *[pltpu.VMEM((rows, groups, n) + tile, jnp.bfloat16) for _, n in chunks],
            dma((windows // FETCH,)),
            dma((groups,)),
            dma((6, cols, 2 * groups)),
            dma((cols, 2 * groups)),
            dma((2, rows, count, groups)),
            dma((rows, count, groups)),
            dma((count,)),
            dma((count,)),
            dma((count,)),
        ],
        compiler_params=pltpu.CompilerParams(
            collective_id=0, has_side_effects=True, vmem_limit_bytes=40 * 2**20),
        cost_estimate=pl.CostEstimate(
            flops=4 * windows * channels * length * bins,
            bytes_accessed=windows * channels * length * 2, transcendentals=0),
    )(pairs, bin_index, records)


def cross_kernel(owned, pairs, count, place, row_set, col_pick, out, ring, sem):
    depth, _, step, channels, _ = ring.shape
    groups = row_set.shape[1]
    chunks = out.shape[4] // step

    def copy(n):
        part = pl.ds((n % chunks) * step, step)
        return pltpu.make_async_copy(
            ring.at[n % depth], out.at[0, 0, n // chunks, :, part], sem.at[n % depth])

    def one(n, _):
        slot = n % depth
        position = place[0] * owned + n // chunks
        i = pairs[0, 0, 0, position]
        live = position < count[0]

        @pl.when(n >= depth)
        def _():
            copy(n - depth).wait()

        @pl.when(live)
        def _():
            for t in range(step):
                k = (n % chunks) * step + t
                a = row_set[i, :, k].reshape(-1, channels)
                b = col_pick[n // chunks, :, k].reshape(a.shape)
                parts = b.astype(jnp.float32).reshape(groups, 2, GROUP, channels)
                turned = jnp.concatenate([-parts[:, 1:], parts[:, :1]], axis=1)
                turned = turned.reshape(a.shape).astype(jnp.bfloat16)
                both = lax.dot_general(
                    a, jnp.concatenate([b, turned], axis=1), (((0,), (0,)), ((), ())),
                    preferred_element_type=jnp.float32)
                ring[slot, 0, t] = both[:, :channels].astype(jnp.bfloat16)
                ring[slot, 1, t] = both[:, channels:].astype(jnp.bfloat16)

        @pl.when(jnp.logical_not(live))
        def _():
            ring[slot] = jnp.zeros(ring.shape[1:], jnp.bfloat16)

        copy(n).start()
        return 0

    total = owned * chunks
    lax.fori_loop(0, total, one, 0)
    for n in range(max(total - depth, 0), total):
        copy(n).wait()


def cross(row_set, col_pick, pairs, count, place):
    owned, groups, bins, entries, channels = col_pick.shape
    step = math.gcd(bins, 8)
    smem = pl.BlockSpec(memory_space=pltpu.SMEM)
    vmem = pl.BlockSpec(memory_space=pltpu.VMEM)
    return pl.pallas_call(
        functools.partial(cross_kernel, owned),
        out_shape=jax.ShapeDtypeStruct(
            (1, 1, owned, 2, bins, channels, channels), jnp.bfloat16),
        in_specs=[smem, smem, smem, vmem, vmem],
        out_specs=pl.BlockSpec(memory_space=pl.ANY),
        scratch_shapes=[
            pltpu.VMEM((4, 2, step, channels, channels), jnp.bfloat16),
            pltpu.SemaphoreType.DMA((4,)),
        ],
        compiler_params=pltpu.CompilerParams(vmem_limit_bytes=40 * 2**20),
        cost_estimate=pl.CostEstimate(
            flops=4 * owned * bins * channels * channels * groups * entries,
            bytes_accessed=4 * owned * bins * channels * channels, transcendentals=0),
    )(pairs, count, place, row_set, col_pick)


def body(records, tile_pairs, tile_count, bin_index):
    rows, cols = lax.axis_size("row"), lax.axis_size("col")
    owned = tile_pairs.shape[2] // lax.axis_size("win")
    pairs = jnp.swapaxes(tile_pairs, 2, 3)
    row_set, col_pick = gather(records, pairs, bin_index, rows, cols, owned)
    place = lax.axis_index("win").astype(jnp.int32).reshape(1)
    return cross(row_set, col_pick, pairs, tile_count.reshape(-1), place)


def solution(mesh):
    return jax.shard_map(
        body,
        mesh=mesh,
        in_specs=(
            P("win", ("row", "col"), None),
            P("row", "col", None, None),
            P("row", "col"),
            P(),
        ),
        out_specs=P("row", "col", "win", None, None, None, None),
        check_vma=False,
    )
```

```python
import functools
import math

import jax
import jax.numpy as jnp
from jax import lax
from jax.experimental import pallas as pl
from jax.experimental.pallas import tpu as pltpu
from jax.sharding import PartitionSpec as P

GROUP = 8
FETCH = 4
AHEAD = 4
UP, DOWN, PARTNER, RIGHT, LEFT, SIBLING = range(6)


def chunk_list(bins):
    size = max(bins // 8, 1)
    ends = list(range(size, bins, size))
    if size > 1:
        ends.append(bins - size // 2)
    ends.append(bins)
    return [(a, b - a) for a, b in zip([0] + ends, ends)]


def cos_sin(phase, length):
    shift = length.bit_length() - 3
    turn = (phase + (1 << shift >> 1)) >> shift
    x = (phase - (turn << shift)).astype(jnp.float32) * (2.0 * math.pi / length)
    y = x * x
    c = 1.0 + y * (-0.5 + y * (1.0 / 24 + y * (-1.0 / 720 + y * (1.0 / 40320))))
    s = x * (1.0 + y * (-1.0 / 6 + y * (1.0 / 120 + y * (-1.0 / 5040 + y * (1.0 / 362880)))))
    odd = (turn & 1) == 1
    cosine, sine = jnp.where(odd, s, c), jnp.where(odd, c, s)
    cosine = jnp.where(((turn + 1) & 2) == 2, -cosine, cosine)
    sine = jnp.where((turn & 2) == 2, -sine, sine)
    return cosine, sine


def fill_table(bin_ref, kcol, table, length):
    assert length & (length - 1) == 0
    bins = kcol.shape[0]
    for k in range(bins):
        kcol[k:k + 1, :] = jnp.full((1, 128), bin_ref[k], jnp.int32)
    for lane in range(0, length, 128):
        samples = lax.broadcasted_iota(jnp.int32, (8, 128), 1) + lane
        taper = 0.5 - 0.5 * cos_sin(samples, length)[0]
        taper = jnp.concatenate([taper] * (bins // 8), axis=0)
        samples = jnp.concatenate([samples] * (bins // 8), axis=0)
        cosine, sine = cos_sin(kcol[...] * samples & (length - 1), length)
        table[:bins, lane:lane + 128] = (taper * cosine).astype(jnp.bfloat16)
        table[bins:, lane:lane + 128] = (-taper * sine).astype(jnp.bfloat16)


def gather_kernel(rows, cols, chunks, pairs_hbm, bin_hbm, rec_hbm, row_set, col_pick,
                  pairs, bin_ref, scalar_sem, kcol, table, rec, spec, own, stage, *rest):
    col = rest[:len(chunks)]
    (rec_sem, local_sem, partner_send, row_send, row_recv, sibling_recv, hop_send, hop_recv,
     pick_sem) = rest[len(chunks):]
    groups, bins = own.shape[0], own.shape[1]
    owned = stage.shape[1]
    w, r, q = lax.axis_index("win"), lax.axis_index("row"), lax.axis_index("col")
    chips = cols // 2
    x = q // 2
    other = 1 - w
    device = {
        UP: (w, r + 1, q), DOWN: (w, r - 1, q), PARTNER: (other, r, q),
        RIGHT: (w, r, q + 2), LEFT: (w, r, q - 2), SIBLING: (w, r, q + 1 - 2 * (q % 2)),
    }
    exists = {
        UP: r < rows - 1, DOWN: r > 0, PARTNER: None,
        RIGHT: x < chips - 1, LEFT: x > 0, SIBLING: None,
    }

    def fetch(i):
        part = pl.ds(i * FETCH, FETCH)
        return pltpu.make_async_copy(rec_hbm.at[part], rec.at[part], rec_sem.at[i])

    scalars = [pltpu.make_async_copy(bin_hbm, bin_ref, scalar_sem.at[0]),
               pltpu.make_async_copy(pairs_hbm, pairs, scalar_sem.at[1])]
    for scalar in scalars:
        scalar.start()
    for i in range(groups * GROUP // FETCH):
        fetch(i).start()

    def guarded(way, f):
        if exists[way] is None:
            f()
        else:
            pl.when(exists[way])(f)

    barrier = pltpu.get_barrier_semaphore()
    for way in range(6):
        guarded(way, lambda way=way: pl.semaphore_signal(
            barrier, inc=1, device_id=device[way], device_id_type=pl.DeviceIdType.MESH))
    ends = sum(exists[way].astype(jnp.int32) for way in (UP, DOWN, RIGHT, LEFT))

    def remote(way, src, dst, send_sem, recv_sem):
        return pltpu.make_async_remote_copy(
            src_ref=src, dst_ref=dst, send_sem=send_sem, recv_sem=recv_sem,
            device_id=device[way], device_id_type=pl.DeviceIdType.MESH)

    def start(way, copy):
        guarded(way, copy.start)

    def row_copy(way, src, slot, part):
        recv = sibling_recv.at[slot // 2] if way == SIBLING else row_recv.at[slot // 2, part]
        return remote(way, src, row_set.at[slot, part], row_send.at[way - RIGHT, slot], recv)

    def row_arrived(slot, part):
        row_copy(RIGHT, row_set.at[slot, part], slot, part).wait_recv()

    def row_relay(cond, slot, part, ways):
        def go():
            row_arrived(slot, part)
            for way in ways:
                start(way, row_copy(way, row_set.at[slot, part], slot, part))

        pl.when(cond)(go)

    def along_x(part):
        for d in range(1, chips):
            row_relay(x - d >= 0, q - 2 * d, part, (RIGHT, SIBLING))
            row_relay(x + d < chips, q + 2 * d, part, (LEFT, SIBLING))

    def to_partner(g):
        return remote(PARTNER, own.at[g], row_set.at[q, groups + g],
                      partner_send.at[0], row_recv.at[q // 2, groups + g])

    def from_partner(g):
        part = groups + g
        row_arrived(q, part)
        for way in (RIGHT, LEFT, SIBLING):
            start(way, row_copy(way, row_set.at[q, part], q, part))

    def rows_done():
        def slot_bytes(way, slot):
            return remote(way, row_set.at[slot], row_set.at[slot],
                          row_send.at[way - RIGHT, slot], sibling_recv.at[slot // 2])

        remote(PARTNER, own, own, partner_send.at[0], partner_send.at[0]).wait_send()
        for way in (RIGHT, LEFT, SIBLING):
            guarded(way, slot_bytes(way, q).wait_send)
        for d in range(1, chips):
            for cond, slot, way in ((x - d >= 0, q - 2 * d, RIGHT), (x + d < chips, q + 2 * d, LEFT)):
                def done(slot=slot, way=way):
                    guarded(way, slot_bytes(way, slot).wait_send)
                    slot_bytes(SIBLING, slot).wait_send()

                pl.when(cond)(done)
        for c in range(chips):
            slot_bytes(SIBLING, 2 * c + 1 - q % 2).wait_recv()

    def hop_copy(way, slot, c, src, dst):
        return remote(way, src, dst, hop_send.at[way, slot],
                      hop_recv.at[slot - (1 if way == DOWN else 0), c])

    def send_own(c, g=None):
        k, n = chunks[c]
        for way in (UP, DOWN):
            if g is None:
                copy = hop_copy(way, r, c, own.at[:, pl.ds(k, n)], col[c].at[r])
            else:
                copy = hop_copy(way, r, c, own.at[g, pl.ds(k, n)], col[c].at[r, g])
            start(way, copy)

    def hop(h, c):
        for cond, slot, way in ((r - h >= 0, r - h, UP), (r + h < rows, r + h, DOWN)):
            def go(slot=slot, way=way):
                copy = hop_copy(way, slot, c, col[c].at[slot], col[c].at[slot])
                copy.wait_recv()
                start(way, copy)

            pl.when(cond)(go)

    def hops_done():
        for slot_cond, slot, way in [(r >= 0, r, UP), (r >= 0, r, DOWN)] + [
                item for h in range(1, rows)
                for item in ((r - h >= 0, r - h, UP), (r + h < rows, r + h, DOWN))]:
            def done(slot=slot, way=way):
                guarded(way, remote(way, own, own, hop_send.at[way, slot],
                                    hop_send.at[way, slot]).wait_send)

            pl.when(slot_cond)(done)

    def pick_copy(part):
        return remote(PARTNER, stage.at[1, :, :, part], col_pick.at[:, pl.ds(groups, groups), part],
                      pick_sem.at[0], pick_sem.at[1])

    def pick_keep(part):
        return pltpu.make_async_copy(
            stage.at[0, :, :, part], col_pick.at[:, pl.ds(0, groups), part], pick_sem.at[2])

    def pick(c):
        k, n = chunks[c]
        for side, half in ((1, other), (0, w)):
            for t in range(owned):
                j = pairs[0, 0, 1, half * owned + t]
                stage[side, t, :, k:k + n] = col[c][j]
            (pick_copy if side else pick_keep)(pl.ds(k, n)).start()

    for scalar in scalars:
        scalar.wait()
    fill_table(bin_ref, kcol, table, rec.shape[2])
    split = min(AHEAD, len(chunks))
    for g in range(groups):
        for i in range(g * GROUP // FETCH, (g + 1) * GROUP // FETCH):
            fetch(i).wait()
            for v in range(i * FETCH, (i + 1) * FETCH):
                s = lax.dot_general(table[...], rec[v], (((1,), (1,)), ((), ())),
                                    preferred_element_type=jnp.float32)
                scale = 1.0 / jnp.sqrt(jnp.mean(s * s, axis=0, keepdims=True) + 1e-06)
                s = s * scale
                first = v % GROUP
                for lane in range(spec.shape[0]):
                    part = s[:, lane * 128:(lane + 1) * 128]
                    spec[lane, pl.ds(first, bins, stride=2 * GROUP), :] = part[:bins]
                    spec[lane, pl.ds(first + GROUP, bins, stride=2 * GROUP), :] = part[bins:]
        for lane in range(spec.shape[0]):
            part = spec[lane].astype(jnp.bfloat16).reshape(bins, 2 * GROUP, 128)
            own[g, :, :, lane * 128:(lane + 1) * 128] = part
            for c, (k, n) in enumerate(chunks):
                col[c][r, g, :, :, lane * 128:(lane + 1) * 128] = part[k:k + n]
        if g == 0:
            pl.semaphore_wait(barrier, 2 + ends)
        send_own(0, g)
        to_partner(g).start()
        for way in (RIGHT, LEFT, SIBLING):
            start(way, row_copy(way, own.at[g], q, g))
        if g == 0:
            for c in range(1, split):
                send_own(c, g)
        elif split > 1:
            send_own(1, g)
    keep = pltpu.make_async_copy(own, row_set.at[q, pl.ds(0, groups)], local_sem.at[0])
    keep.start()

    last = len(chunks) + rows - 2
    row_work = {}
    for g in range(groups):
        row_work[2 + 2 * g] = lambda g=g: from_partner(g)
        row_work[3 + 2 * g] = lambda g=g: along_x(g)
        row_work[3 + 2 * groups + g] = lambda g=g: along_x(groups + g)
    for step in range(max(last, 3 + 3 * groups)):
        if 2 + step < len(chunks):
            if 2 + step < split:
                for g in range(1, groups):
                    send_own(2 + step, g)
            else:
                send_own(2 + step)
        for h in range(1, rows):
            if 0 <= step - h + 1 < len(chunks):
                hop(h, step - h + 1)
        if 0 <= step - rows + 2 < len(chunks):
            pick(step - rows + 2)
        if step in row_work:
            row_work[step]()

    every = pl.ds(0, bins)
    rows_done()
    hops_done()
    pick_copy(every).wait()
    pick_keep(every).wait()
    keep.wait()


def gather(records, pairs, bin_index, rows, cols, owned):
    windows, channels, length = records.shape
    groups = windows // GROUP
    bins = bin_index.shape[0]
    chunks = chunk_list(bins)
    count = len(chunks)
    hbm = pl.BlockSpec(memory_space=pl.ANY)
    dma = pltpu.SemaphoreType.DMA
    tile = (2 * GROUP, channels)
    return pl.pallas_call(
        functools.partial(gather_kernel, rows, cols, chunks),
        out_shape=(
            jax.ShapeDtypeStruct((cols, 2 * groups, bins) + tile, jnp.bfloat16),
            jax.ShapeDtypeStruct((owned, 2 * groups, bins) + tile, jnp.bfloat16)),
        in_specs=[pl.BlockSpec(memory_space=pltpu.HBM)] * 2 + [hbm],
        out_specs=(hbm, hbm),
        scratch_shapes=[
            pltpu.SMEM(pairs.shape, jnp.int32),
            pltpu.SMEM((bins,), jnp.int32),
            dma((2,)),
            pltpu.VMEM((bins, 128), jnp.int32),
            pltpu.VMEM((2 * bins, length), jnp.bfloat16),
            pltpu.VMEM(records.shape, jnp.bfloat16),
            pltpu.VMEM((channels // 128, 2 * bins * GROUP, 128), jnp.float32),
            pltpu.VMEM((groups, bins) + tile, jnp.bfloat16),
            pltpu.VMEM((2, owned, groups, bins) + tile, jnp.bfloat16),
            *[pltpu.VMEM((rows, groups, n) + tile, jnp.bfloat16) for _, n in chunks],
            dma((windows // FETCH,)),
            dma((1,)),
            dma((1,)),
            dma((3, cols)),
            dma((cols // 2, 2 * groups)),
            dma((cols // 2,)),
            dma((2, rows)),
            dma((rows - 1, count)),
            dma((3,)),
        ],
        compiler_params=pltpu.CompilerParams(
            collective_id=0, has_side_effects=True, vmem_limit_bytes=40 * 2**20),
        cost_estimate=pl.CostEstimate(
            flops=4 * windows * channels * length * bins,
            bytes_accessed=windows * channels * length * 2, transcendentals=0),
    )(pairs, bin_index, records)


def cross_kernel(owned, pairs, count, place, row_set, col_pick, out, ring, sem):
    depth, _, step, channels, _ = ring.shape
    groups = row_set.shape[1]
    chunks = out.shape[4] // step

    def copy(n):
        part = pl.ds((n % chunks) * step, step)
        return pltpu.make_async_copy(
            ring.at[n % depth], out.at[0, 0, n // chunks, :, part], sem.at[n % depth])

    def one(n, _):
        slot = n % depth
        position = place[0] * owned + n // chunks
        i = pairs[0, 0, 0, position]
        live = position < count[0]

        @pl.when(n >= depth)
        def _():
            copy(n - depth).wait()

        @pl.when(live)
        def _():
            for t in range(step):
                k = (n % chunks) * step + t
                a = row_set[i, :, k].reshape(-1, channels)
                b = col_pick[n // chunks, :, k].reshape(a.shape)
                parts = b.astype(jnp.float32).reshape(groups, 2, GROUP, channels)
                turned = jnp.concatenate([-parts[:, 1:], parts[:, :1]], axis=1)
                turned = turned.reshape(a.shape).astype(jnp.bfloat16)
                both = lax.dot_general(
                    a, jnp.concatenate([b, turned], axis=1), (((0,), (0,)), ((), ())),
                    preferred_element_type=jnp.float32)
                ring[slot, 0, t] = both[:, :channels].astype(jnp.bfloat16)
                ring[slot, 1, t] = both[:, channels:].astype(jnp.bfloat16)

        @pl.when(jnp.logical_not(live))
        def _():
            ring[slot] = jnp.zeros(ring.shape[1:], jnp.bfloat16)

        copy(n).start()
        return 0

    total = owned * chunks
    lax.fori_loop(0, total, one, 0)
    for n in range(max(total - depth, 0), total):
        copy(n).wait()


def cross(row_set, col_pick, pairs, count, place):
    owned, groups, bins, entries, channels = col_pick.shape
    step = math.gcd(bins, 8)
    smem = pl.BlockSpec(memory_space=pltpu.SMEM)
    vmem = pl.BlockSpec(memory_space=pltpu.VMEM)
    return pl.pallas_call(
        functools.partial(cross_kernel, owned),
        out_shape=jax.ShapeDtypeStruct(
            (1, 1, owned, 2, bins, channels, channels), jnp.bfloat16),
        in_specs=[smem, smem, smem, vmem, vmem],
        out_specs=pl.BlockSpec(memory_space=pl.ANY),
        scratch_shapes=[
            pltpu.VMEM((4, 2, step, channels, channels), jnp.bfloat16),
            pltpu.SemaphoreType.DMA((4,)),
        ],
        compiler_params=pltpu.CompilerParams(vmem_limit_bytes=40 * 2**20),
        cost_estimate=pl.CostEstimate(
            flops=4 * owned * bins * channels * channels * groups * entries,
            bytes_accessed=4 * owned * bins * channels * channels, transcendentals=0),
    )(pairs, count, place, row_set, col_pick)


def body(records, tile_pairs, tile_count, bin_index):
    rows, cols = lax.axis_size("row"), lax.axis_size("col")
    owned = tile_pairs.shape[2] // lax.axis_size("win")
    pairs = jnp.swapaxes(tile_pairs, 2, 3)
    row_set, col_pick = gather(records, pairs, bin_index, rows, cols, owned)
    place = lax.axis_index("win").astype(jnp.int32).reshape(1)
    return cross(row_set, col_pick, pairs, tile_count.reshape(-1), place)


def solution(mesh):
    return jax.shard_map(
        body,
        mesh=mesh,
        in_specs=(
            P("win", ("row", "col"), None),
            P("row", "col", None, None),
            P("row", "col"),
            P(),
        ),
        out_specs=P("row", "col", "win", None, None, None, None),
        check_vma=False,
    )
```

```python
import functools
import math

import jax
import jax.numpy as jnp
from jax import lax
from jax.experimental import pallas as pl
from jax.experimental.pallas import tpu as pltpu
from jax.sharding import PartitionSpec as P

GROUP = 8
FETCH = 4
AHEAD = 5
BOTH = 3
WINDOW = 2
UP, DOWN, PARTNER, RIGHT, LEFT, SIBLING, CROSS_UP, CROSS_DOWN = range(8)


def chunk_list(bins):
    size = max(bins // 8, 1)
    return [(k, min(size, bins - k)) for k in range(0, bins, size)]


def cos_sin(phase, length):
    shift = length.bit_length() - 3
    turn = (phase + (1 << shift >> 1)) >> shift
    x = (phase - (turn << shift)).astype(jnp.float32) * (2.0 * math.pi / length)
    y = x * x
    c = 1.0 + y * (-0.5 + y * (1.0 / 24 + y * (-1.0 / 720 + y * (1.0 / 40320))))
    s = x * (1.0 + y * (-1.0 / 6 + y * (1.0 / 120 + y * (-1.0 / 5040 + y * (1.0 / 362880)))))
    odd = (turn & 1) == 1
    cosine, sine = jnp.where(odd, s, c), jnp.where(odd, c, s)
    cosine = jnp.where(((turn + 1) & 2) == 2, -cosine, cosine)
    sine = jnp.where((turn & 2) == 2, -sine, sine)
    return cosine, sine


def fill_table(bin_ref, kcol, table, length):
    assert length & (length - 1) == 0
    bins = kcol.shape[0]
    for k in range(bins):
        kcol[k:k + 1, :] = jnp.full((1, 128), bin_ref[k], jnp.int32)
    for lane in range(0, length, 128):
        samples = lax.broadcasted_iota(jnp.int32, (8, 128), 1) + lane
        taper = 0.5 - 0.5 * cos_sin(samples, length)[0]
        taper = jnp.concatenate([taper] * (bins // 8), axis=0)
        samples = jnp.concatenate([samples] * (bins // 8), axis=0)
        cosine, sine = cos_sin(kcol[...] * samples & (length - 1), length)
        table[:bins, lane:lane + 128] = (taper * cosine).astype(jnp.bfloat16)
        table[bins:, lane:lane + 128] = (-taper * sine).astype(jnp.bfloat16)


def gather_kernel(rows, cols, chunks, pairs_hbm, bin_hbm, rec_hbm, row_set, col_pick,
                  pairs, bin_ref, scalar_sem, kcol, table, rec, spec, own, stage,
                  end_stage, end_arrived, end_pairs, *rest):
    col = rest[:len(chunks)]
    (rec_sem, local_sem, partner_send, row_send, row_recv, sibling_recv, hop_send, relay_send, hop_recv,
     pick_sem, pair_sem, end_send, end_recv) = rest[len(chunks):]
    groups, bins = own.shape[0], own.shape[1]
    owned = stage.shape[1]
    w, r, q = lax.axis_index("win"), lax.axis_index("row"), lax.axis_index("col")
    chips = cols // 2
    x = q // 2
    other = 1 - w
    device = {
        UP: (w, r + 1, q), DOWN: (w, r - 1, q), PARTNER: (other, r, q),
        RIGHT: (w, r, q + 2), LEFT: (w, r, q - 2), SIBLING: (w, r, q + 1 - 2 * (q % 2)),
        CROSS_UP: (other, r + 1, q), CROSS_DOWN: (other, r - 1, q),
    }
    exists = {
        UP: r < rows - 1, DOWN: r > 0, PARTNER: None,
        RIGHT: x < chips - 1, LEFT: x > 0, SIBLING: None,
        CROSS_UP: (r == 0) | (r == rows - 2), CROSS_DOWN: (r == 1) | (r == rows - 1),
    }

    last_chunk = len(chunks) - 1
    early = chunks[last_chunk][0]
    inner = (r > 0) & (r < rows - 1)
    to_end = {UP: r == rows - 2, DOWN: r == 1}

    def fetch(i):
        part = pl.ds(i * FETCH, FETCH)
        return pltpu.make_async_copy(rec_hbm.at[part], rec.at[part], rec_sem.at[i])

    scalars = [pltpu.make_async_copy(bin_hbm, bin_ref, scalar_sem.at[0]),
               pltpu.make_async_copy(pairs_hbm, pairs, scalar_sem.at[1])]
    for scalar in scalars:
        scalar.start()
    for i in range(groups * GROUP // FETCH):
        fetch(i).start()

    def guarded(way, f):
        if exists[way] is None:
            f()
        else:
            pl.when(exists[way])(f)

    barrier = pltpu.get_barrier_semaphore()
    for way in range(8):
        guarded(way, lambda way=way: pl.semaphore_signal(
            barrier, inc=1, device_id=device[way], device_id_type=pl.DeviceIdType.MESH))
    ends = sum(exists[way].astype(jnp.int32)
               for way in (UP, DOWN, RIGHT, LEFT, CROSS_UP, CROSS_DOWN))

    def remote(way, src, dst, send_sem, recv_sem):
        return pltpu.make_async_remote_copy(
            src_ref=src, dst_ref=dst, send_sem=send_sem, recv_sem=recv_sem,
            device_id=device[way], device_id_type=pl.DeviceIdType.MESH)

    def start(way, copy):
        guarded(way, copy.start)

    def row_copy(way, src, slot, part):
        recv = sibling_recv.at[slot // 2] if way == SIBLING else row_recv.at[slot // 2, part]
        return remote(way, src, row_set.at[slot, part], row_send.at[way - RIGHT, slot], recv)

    def row_arrived(slot, part):
        row_copy(RIGHT, row_set.at[slot, part], slot, part).wait_recv()

    def row_relay(cond, slot, part, ways):
        def go():
            row_arrived(slot, part)
            for way in ways:
                start(way, row_copy(way, row_set.at[slot, part], slot, part))

        pl.when(cond)(go)

    def along_x(part):
        for d in range(1, chips):
            row_relay(x - d >= 0, q - 2 * d, part, (RIGHT, SIBLING))
            row_relay(x + d < chips, q + 2 * d, part, (LEFT, SIBLING))

    def to_partner(g):
        return remote(PARTNER, own.at[g], row_set.at[q, groups + g],
                      partner_send.at[0], row_recv.at[q // 2, groups + g])

    def from_partner(g):
        part = groups + g
        row_arrived(q, part)
        for way in (RIGHT, LEFT, SIBLING):
            start(way, row_copy(way, row_set.at[q, part], q, part))

    def rows_done():
        def slot_bytes(way, slot):
            return remote(way, row_set.at[slot], row_set.at[slot],
                          row_send.at[way - RIGHT, slot], sibling_recv.at[slot // 2])

        remote(PARTNER, own, own, partner_send.at[0], partner_send.at[0]).wait_send()
        for way in (RIGHT, LEFT, SIBLING):
            guarded(way, slot_bytes(way, q).wait_send)
        for d in range(1, chips):
            for cond, slot, way in ((x - d >= 0, q - 2 * d, RIGHT), (x + d < chips, q + 2 * d, LEFT)):
                def done(slot=slot, way=way):
                    guarded(way, slot_bytes(way, slot).wait_send)
                    slot_bytes(SIBLING, slot).wait_send()

                pl.when(cond)(done)
        for c in range(chips):
            slot_bytes(SIBLING, 2 * c + 1 - q % 2).wait_recv()

    def hop_copy(way, slot, c, src, dst, sem):
        return remote(way, src, dst, sem, hop_recv.at[slot - (1 if way == DOWN else 0), c])

    def start_hop(way, c, copy, wait=False):
        goes = exists[way]
        if c == last_chunk:
            goes = goes & jnp.logical_not(to_end[way])
        pl.when(goes)(copy.wait_send if wait else copy.start)

    def send_own(c, g, to_ends):
        k, n = chunks[c]
        for way in (UP, DOWN):
            goes = to_end[way] if to_ends else exists[way] & jnp.logical_not(to_end[way])
            if g is None:
                copy = hop_copy(way, r, c, own.at[:, pl.ds(k, n)], col[c].at[r], hop_send.at[way])
            else:
                copy = hop_copy(way, r, c, own.at[g, pl.ds(k, n)], col[c].at[r, g],
                                hop_send.at[way])
            pl.when(goes)(copy.start)

    def relay(h, way, slot, c):
        return hop_copy(way, slot, c, col[c].at[slot], col[c].at[slot],
                        relay_send.at[way, h - 1, c % WINDOW])

    def ways(h):
        return (r - h >= 0, r - h, UP), (r + h < rows, r + h, DOWN)

    def hop(h, c):
        for cond, slot, way in ways(h):
            def go(slot=slot, way=way):
                relay(h, way, slot, c).wait_recv()
                if c >= WINDOW:
                    start_hop(way, c, relay(h, way, slot, c - WINDOW), True)
                start_hop(way, c, relay(h, way, slot, c))

            pl.when(cond & inner if c == last_chunk else cond)(go)

    def relays_sent(to_ends):
        for h in range(1, rows):
            for cond, slot, way in ways(h):
                goes = to_end[way] if to_ends else exists[way] & jnp.logical_not(to_end[way])
                top = last_chunk if to_ends else len(chunks)
                for c in range(max(top - WINDOW, 0), top):
                    pl.when(cond & goes)(relay(h, way, slot, c).wait_send)

    def hops_done():
        relays_sent(False)
        for way in (UP, DOWN):
            for end, part in ((False, own), (True, own.at[:, pl.ds(0, early)])):
                goes = to_end[way] if end else exists[way] & jnp.logical_not(to_end[way])
                pl.when(goes)(remote(way, part, part, hop_send.at[way], hop_send.at[way]).wait_send)

    sides = ((0, r == 1, r == 0, UP, DOWN, CROSS_DOWN),
             (1, r == rows - 2, r == rows - 1, DOWN, UP, CROSS_UP))

    def pair_copy(side, way):
        return remote(way, pairs_hbm, end_arrived.at[side], pair_sem.at[0], pair_sem.at[1 + side])

    def send_pairs():
        for side, _, end, way, _, _ in sides:
            pl.when(end)(pair_copy(side, way).start)

    def take_pairs():
        for side, serves, end, way, _, _ in sides:
            def take(side=side, way=way):
                pair_copy(side, way).wait_recv()
                keep = pltpu.make_async_copy(end_arrived.at[side], end_pairs.at[side], pair_sem.at[3])
                keep.start()
                keep.wait()

            pl.when(end)(pair_copy(side, way).wait_send)
            pl.when(serves)(take)

    def end_copy(side, far, way):
        return remote(way, end_stage.at[side, far],
                      col_pick.at[:, pl.ds(far * groups, groups), pl.ds(early, bins - early)],
                      end_send.at[side, far], end_recv.at[far])

    def serve_ends():
        for side, serves, _, _, near, cross_way in sides:
            def serve(side=side, near=near, cross_way=cross_way):
                for far, half, way in ((1, other, cross_way), (0, w, near)):
                    for t in range(owned):
                        j = end_pairs[side, 0, 0, 1, half * owned + t]
                        end_stage[side, far, t] = col[last_chunk][j]
                    end_copy(side, far, way).start()

            pl.when(serves)(serve)

    def ends_done():
        for side, serves, end, _, near, cross_way in sides:
            for far, way in ((1, cross_way), (0, near)):
                copy = end_copy(side, far, way)
                pl.when(serves)(copy.wait_send)
                pl.when(end)(copy.wait_recv)

    def pick_copy(part):
        return remote(PARTNER, stage.at[1, :, :, part], col_pick.at[:, pl.ds(groups, groups), part],
                      pick_sem.at[0], pick_sem.at[1])

    def pick_keep(part):
        return pltpu.make_async_copy(
            stage.at[0, :, :, part], col_pick.at[:, pl.ds(0, groups), part], pick_sem.at[2])

    def pick(c):
        if c == last_chunk:
            relays_sent(True)
            serve_ends()
            pl.when(inner)(lambda: pick_chunk(c))
        else:
            pick_chunk(c)

    def pick_chunk(c):
        k, n = chunks[c]
        for side, half in ((1, other), (0, w)):
            for t in range(owned):
                j = pairs[0, 0, 1, half * owned + t]
                stage[side, t, :, k:k + n] = col[c][j]
            (pick_copy if side else pick_keep)(pl.ds(k, n)).start()

    for scalar in scalars:
        scalar.wait()
    fill_table(bin_ref, kcol, table, rec.shape[2])
    ahead, both = min(AHEAD, last_chunk), min(BOTH, last_chunk)
    for g in range(groups):
        for i in range(g * GROUP // FETCH, (g + 1) * GROUP // FETCH):
            fetch(i).wait()
            for v in range(i * FETCH, (i + 1) * FETCH):
                s = lax.dot_general(table[...], rec[v], (((1,), (1,)), ((), ())),
                                    preferred_element_type=jnp.float32)
                scale = 1.0 / jnp.sqrt(jnp.mean(s * s, axis=0, keepdims=True) + 1e-06)
                s = s * scale
                first = v % GROUP
                for lane in range(spec.shape[0]):
                    part = s[:, lane * 128:(lane + 1) * 128]
                    spec[lane, pl.ds(first, bins, stride=2 * GROUP), :] = part[:bins]
                    spec[lane, pl.ds(first + GROUP, bins, stride=2 * GROUP), :] = part[bins:]
        for lane in range(spec.shape[0]):
            part = spec[lane].astype(jnp.bfloat16).reshape(bins, 2 * GROUP, 128)
            own[g, :, :, lane * 128:(lane + 1) * 128] = part
            for c, (k, n) in enumerate(chunks):
                col[c][r, g, :, :, lane * 128:(lane + 1) * 128] = part[k:k + n]
        if g == 0:
            pl.semaphore_wait(barrier, 2 + ends)
            send_pairs()
        for c in range(2):
            send_own(c, g, False)
            send_own(c, g, True)
        to_partner(g).start()
        for way in (RIGHT, LEFT, SIBLING):
            start(way, row_copy(way, own.at[g], q, g))
        for c in range(2, ahead if g == 0 else both):
            send_own(c, g, True)
    keep = pltpu.make_async_copy(own, row_set.at[q, pl.ds(0, groups)], local_sem.at[0])
    keep.start()

    last = len(chunks) + rows - 2
    row_work = {}
    for g in range(groups):
        row_work[2 + 2 * g] = lambda g=g: from_partner(g)
        row_work[3 + 2 * g] = lambda g=g: along_x(g)
        row_work[3 + 2 * groups + g] = lambda g=g: along_x(groups + g)
    for step in range(max(last, 3 + 3 * groups)):
        c = 2 + step
        if c < len(chunks):
            send_own(c, None, False)
        if both <= c < ahead:
            for g in range(1, groups):
                send_own(c, g, True)
        elif ahead <= c < last_chunk:
            send_own(c, None, True)
        for h in range(1, rows):
            if 0 <= step - h + 1 < len(chunks):
                hop(h, step - h + 1)
        if 0 <= step - rows + 2 < len(chunks):
            pick(step - rows + 2)
        if step == 1:
            take_pairs()
        if step in row_work:
            row_work[step]()

    rows_done()
    hops_done()
    for n, goes in ((bins, inner), (early, jnp.logical_not(inner))):
        def picks_done(n=n):
            pick_copy(pl.ds(0, n)).wait()
            pick_keep(pl.ds(0, n)).wait()

        pl.when(goes)(picks_done)
    ends_done()
    keep.wait()


def gather(records, pairs, bin_index, rows, cols, owned):
    windows, channels, length = records.shape
    groups = windows // GROUP
    bins = bin_index.shape[0]
    chunks = chunk_list(bins)
    count = len(chunks)
    hbm = pl.BlockSpec(memory_space=pl.ANY)
    dma = pltpu.SemaphoreType.DMA
    tile = (2 * GROUP, channels)
    return pl.pallas_call(
        functools.partial(gather_kernel, rows, cols, chunks),
        out_shape=(
            jax.ShapeDtypeStruct((cols, 2 * groups, bins) + tile, jnp.bfloat16),
            jax.ShapeDtypeStruct((owned, 2 * groups, bins) + tile, jnp.bfloat16)),
        in_specs=[pl.BlockSpec(memory_space=pltpu.HBM)] * 2 + [hbm],
        out_specs=(hbm, hbm),
        scratch_shapes=[
            pltpu.SMEM(pairs.shape, jnp.int32),
            pltpu.SMEM((bins,), jnp.int32),
            dma((2,)),
            pltpu.VMEM((bins, 128), jnp.int32),
            pltpu.VMEM((2 * bins, length), jnp.bfloat16),
            pltpu.VMEM(records.shape, jnp.bfloat16),
            pltpu.VMEM((channels // 128, 2 * bins * GROUP, 128), jnp.float32),
            pltpu.VMEM((groups, bins) + tile, jnp.bfloat16),
            pltpu.VMEM((2, owned, groups, bins) + tile, jnp.bfloat16),
            pltpu.VMEM((2, 2, owned, groups, chunks[-1][1]) + tile, jnp.bfloat16),
            pltpu.VMEM((2,) + pairs.shape, jnp.int32),
            pltpu.SMEM((2,) + pairs.shape, jnp.int32),
            *[pltpu.VMEM((rows, groups, n) + tile, jnp.bfloat16) for _, n in chunks],
            dma((windows // FETCH,)),
            dma((1,)),
            dma((1,)),
            dma((3, cols)),
            dma((cols // 2, 2 * groups)),
            dma((cols // 2,)),
            dma((2,)),
            dma((2, rows - 1, WINDOW)),
            dma((rows - 1, count)),
            dma((3,)),
            dma((4,)),
            dma((2, 2)),
            dma((2,)),
        ],
        compiler_params=pltpu.CompilerParams(
            collective_id=0, has_side_effects=True, vmem_limit_bytes=40 * 2**20),
        cost_estimate=pl.CostEstimate(
            flops=4 * windows * channels * length * bins,
            bytes_accessed=windows * channels * length * 2, transcendentals=0),
    )(pairs, bin_index, records)


def cross_kernel(owned, pairs, count, place, row_set, col_pick, out, ring, sem):
    depth, _, step, channels, _ = ring.shape
    groups = row_set.shape[1]
    chunks = out.shape[4] // step

    def copy(n):
        part = pl.ds((n % chunks) * step, step)
        return pltpu.make_async_copy(
            ring.at[n % depth], out.at[0, 0, n // chunks, :, part], sem.at[n % depth])

    def one(n, _):
        slot = n % depth
        position = place[0] * owned + n // chunks
        i = pairs[0, 0, 0, position]
        live = position < count[0]

        @pl.when(n >= depth)
        def _():
            copy(n - depth).wait()

        @pl.when(live)
        def _():
            for t in range(step):
                k = (n % chunks) * step + t
                a = row_set[i, :, k].reshape(-1, channels)
                b = col_pick[n // chunks, :, k].reshape(a.shape)
                parts = b.astype(jnp.float32).reshape(groups, 2, GROUP, channels)
                turned = jnp.concatenate([-parts[:, 1:], parts[:, :1]], axis=1)
                turned = turned.reshape(a.shape).astype(jnp.bfloat16)
                both = lax.dot_general(
                    a, jnp.concatenate([b, turned], axis=1), (((0,), (0,)), ((), ())),
                    preferred_element_type=jnp.float32)
                ring[slot, 0, t] = both[:, :channels].astype(jnp.bfloat16)
                ring[slot, 1, t] = both[:, channels:].astype(jnp.bfloat16)

        @pl.when(jnp.logical_not(live))
        def _():
            ring[slot] = jnp.zeros(ring.shape[1:], jnp.bfloat16)

        copy(n).start()
        return 0

    total = owned * chunks
    lax.fori_loop(0, total, one, 0)
    for n in range(max(total - depth, 0), total):
        copy(n).wait()


def cross(row_set, col_pick, pairs, count, place):
    owned, groups, bins, entries, channels = col_pick.shape
    step = math.gcd(bins, 8)
    smem = pl.BlockSpec(memory_space=pltpu.SMEM)
    vmem = pl.BlockSpec(memory_space=pltpu.VMEM)
    return pl.pallas_call(
        functools.partial(cross_kernel, owned),
        out_shape=jax.ShapeDtypeStruct(
            (1, 1, owned, 2, bins, channels, channels), jnp.bfloat16),
        in_specs=[smem, smem, smem, vmem, vmem],
        out_specs=pl.BlockSpec(memory_space=pl.ANY),
        scratch_shapes=[
            pltpu.VMEM((4, 2, step, channels, channels), jnp.bfloat16),
            pltpu.SemaphoreType.DMA((4,)),
        ],
        compiler_params=pltpu.CompilerParams(vmem_limit_bytes=40 * 2**20),
        cost_estimate=pl.CostEstimate(
            flops=4 * owned * bins * channels * channels * groups * entries,
            bytes_accessed=4 * owned * bins * channels * channels, transcendentals=0),
    )(pairs, count, place, row_set, col_pick)


def body(records, tile_pairs, tile_count, bin_index):
    rows, cols = lax.axis_size("row"), lax.axis_size("col")
    owned = tile_pairs.shape[2] // lax.axis_size("win")
    pairs = jnp.swapaxes(tile_pairs, 2, 3)
    row_set, col_pick = gather(records, pairs, bin_index, rows, cols, owned)
    place = lax.axis_index("win").astype(jnp.int32).reshape(1)
    return cross(row_set, col_pick, pairs, tile_count.reshape(-1), place)


def solution(mesh):
    return jax.shard_map(
        body,
        mesh=mesh,
        in_specs=(
            P("win", ("row", "col"), None),
            P("row", "col", None, None),
            P("row", "col"),
            P(),
        ),
        out_specs=P("row", "col", "win", None, None, None, None),
        check_vma=False,
    )
```

```python
import functools
import math

import jax
import jax.numpy as jnp
from jax import lax
from jax.experimental import pallas as pl
from jax.experimental.pallas import tpu as pltpu
from jax.sharding import PartitionSpec as P

GROUP = 8
FETCH = 4
AHEAD = 5
BOTH = 3
WINDOW = 2
UP, DOWN, PARTNER, RIGHT, LEFT, SIBLING, CROSS_UP, CROSS_DOWN = range(8)


def chunk_list(bins):
    size = max(bins // 8, 1)
    starts = list(range(0, 6 * size, size))
    if size > 3:
        starts += [6 * size - size // 2, 6 * size + size // 4]
    return [(a, b - a) for a, b in zip(starts, starts[1:] + [bins])]


def cos_sin(phase, length):
    shift = length.bit_length() - 3
    turn = (phase + (1 << shift >> 1)) >> shift
    x = (phase - (turn << shift)).astype(jnp.float32) * (2.0 * math.pi / length)
    y = x * x
    c = 1.0 + y * (-0.5 + y * (1.0 / 24 + y * (-1.0 / 720 + y * (1.0 / 40320))))
    s = x * (1.0 + y * (-1.0 / 6 + y * (1.0 / 120 + y * (-1.0 / 5040 + y * (1.0 / 362880)))))
    odd = (turn & 1) == 1
    cosine, sine = jnp.where(odd, s, c), jnp.where(odd, c, s)
    cosine = jnp.where(((turn + 1) & 2) == 2, -cosine, cosine)
    sine = jnp.where((turn & 2) == 2, -sine, sine)
    return cosine, sine


def fill_table(facts, kcol, table, length):
    assert length & (length - 1) == 0
    bins = kcol.shape[0]
    for k in range(bins):
        kcol[k:k + 1, :] = jnp.full((1, 128), facts[2, k], jnp.int32)
    for lane in range(0, length, 128):
        samples = lax.broadcasted_iota(jnp.int32, (8, 128), 1) + lane
        taper = 0.5 - 0.5 * cos_sin(samples, length)[0]
        taper = jnp.concatenate([taper] * (bins // 8), axis=0)
        samples = jnp.concatenate([samples] * (bins // 8), axis=0)
        cosine, sine = cos_sin(kcol[...] * samples & (length - 1), length)
        table[:bins, lane:lane + 128] = (taper * cosine).astype(jnp.bfloat16)
        table[bins:, lane:lane + 128] = (-taper * sine).astype(jnp.bfloat16)


def gather_kernel(rows, cols, chunks, facts_hbm, rec_hbm, row_set, col_pick,
                  facts, facts_sem, kcol, table, rec, spec, own, stage,
                  end_stage, end_arrived, end_pairs, *rest):
    col = rest[:len(chunks)]
    (rec_sem, local_sem, partner_send, row_send, row_recv, sibling_recv, hop_send, relay_send, hop_recv,
     pick_sem, pair_sem, end_send, end_recv) = rest[len(chunks):]
    groups, bins = own.shape[0], own.shape[1]
    owned = stage.shape[1]
    w, r, q = lax.axis_index("win"), lax.axis_index("row"), lax.axis_index("col")
    chips = cols // 2
    x = q // 2
    other = 1 - w
    device = {
        UP: (w, r + 1, q), DOWN: (w, r - 1, q), PARTNER: (other, r, q),
        RIGHT: (w, r, q + 2), LEFT: (w, r, q - 2), SIBLING: (w, r, q + 1 - 2 * (q % 2)),
        CROSS_UP: (other, r + 1, q), CROSS_DOWN: (other, r - 1, q),
    }
    exists = {
        UP: r < rows - 1, DOWN: r > 0, PARTNER: None,
        RIGHT: x < chips - 1, LEFT: x > 0, SIBLING: None,
        CROSS_UP: (r == 0) | (r == rows - 2), CROSS_DOWN: (r == 1) | (r == rows - 1),
    }

    last_chunk = len(chunks) - 1
    early = chunks[last_chunk][0]
    inner = (r > 0) & (r < rows - 1)
    to_end = {UP: r == rows - 2, DOWN: r == 1}

    def fetch(i):
        part = pl.ds(i * FETCH, FETCH)
        return pltpu.make_async_copy(rec_hbm.at[part], rec.at[part], rec_sem.at[i])

    get_facts = pltpu.make_async_copy(facts_hbm, facts, facts_sem.at[0])
    get_facts.start()
    for i in range(groups * GROUP // FETCH):
        fetch(i).start()

    def guarded(way, f):
        if exists[way] is None:
            f()
        else:
            pl.when(exists[way])(f)

    barrier = pltpu.get_barrier_semaphore()
    for way in range(8):
        guarded(way, lambda way=way: pl.semaphore_signal(
            barrier, inc=1, device_id=device[way], device_id_type=pl.DeviceIdType.MESH))
    ends = sum(exists[way].astype(jnp.int32)
               for way in (UP, DOWN, RIGHT, LEFT, CROSS_UP, CROSS_DOWN))

    def remote(way, src, dst, send_sem, recv_sem):
        return pltpu.make_async_remote_copy(
            src_ref=src, dst_ref=dst, send_sem=send_sem, recv_sem=recv_sem,
            device_id=device[way], device_id_type=pl.DeviceIdType.MESH)

    def start(way, copy):
        guarded(way, copy.start)

    def row_copy(way, src, slot, part):
        recv = sibling_recv.at[slot // 2] if way == SIBLING else row_recv.at[slot // 2, part]
        return remote(way, src, row_set.at[slot, part], row_send.at[way - RIGHT, slot], recv)

    def row_arrived(slot, part):
        row_copy(RIGHT, row_set.at[slot, part], slot, part).wait_recv()

    def row_relay(cond, slot, part, ways):
        def go():
            row_arrived(slot, part)
            for way in ways:
                start(way, row_copy(way, row_set.at[slot, part], slot, part))

        pl.when(cond)(go)

    def along_x(part):
        for d in range(1, chips):
            row_relay(x - d >= 0, q - 2 * d, part, (RIGHT, SIBLING))
            row_relay(x + d < chips, q + 2 * d, part, (LEFT, SIBLING))

    def to_partner(g):
        return remote(PARTNER, own.at[g], row_set.at[q, groups + g],
                      partner_send.at[0], row_recv.at[q // 2, groups + g])

    def from_partner(g):
        part = groups + g
        row_arrived(q, part)
        for way in (RIGHT, LEFT, SIBLING):
            start(way, row_copy(way, row_set.at[q, part], q, part))

    def rows_done():
        def slot_bytes(way, slot):
            return remote(way, row_set.at[slot], row_set.at[slot],
                          row_send.at[way - RIGHT, slot], sibling_recv.at[slot // 2])

        remote(PARTNER, own, own, partner_send.at[0], partner_send.at[0]).wait_send()
        for way in (RIGHT, LEFT, SIBLING):
            guarded(way, slot_bytes(way, q).wait_send)
        for d in range(1, chips):
            for cond, slot, way in ((x - d >= 0, q - 2 * d, RIGHT), (x + d < chips, q + 2 * d, LEFT)):
                def done(slot=slot, way=way):
                    guarded(way, slot_bytes(way, slot).wait_send)
                    slot_bytes(SIBLING, slot).wait_send()

                pl.when(cond)(done)
        for c in range(chips):
            slot_bytes(SIBLING, 2 * c + 1 - q % 2).wait_recv()

    def hop_copy(way, slot, c, src, dst, sem):
        return remote(way, src, dst, sem, hop_recv.at[slot - (1 if way == DOWN else 0), c])

    def start_hop(way, c, copy, wait=False):
        goes = exists[way]
        if c == last_chunk:
            goes = goes & jnp.logical_not(to_end[way])
        pl.when(goes)(copy.wait_send if wait else copy.start)

    def send_own(c, g, to_ends):
        k, n = chunks[c]
        for way in (UP, DOWN):
            goes = to_end[way] if to_ends else exists[way] & jnp.logical_not(to_end[way])
            if g is None:
                copy = hop_copy(way, r, c, own.at[:, pl.ds(k, n)], col[c].at[r], hop_send.at[way])
            else:
                copy = hop_copy(way, r, c, own.at[g, pl.ds(k, n)], col[c].at[r, g],
                                hop_send.at[way])
            pl.when(goes)(copy.start)

    def relay(h, way, slot, c):
        return hop_copy(way, slot, c, col[c].at[slot], col[c].at[slot],
                        relay_send.at[way, h - 1, c % WINDOW])

    def ways(h):
        return (r - h >= 0, r - h, UP), (r + h < rows, r + h, DOWN)

    def hop(h, c):
        for cond, slot, way in ways(h):
            def go(slot=slot, way=way):
                relay(h, way, slot, c).wait_recv()
                if c >= WINDOW:
                    start_hop(way, c, relay(h, way, slot, c - WINDOW), True)
                start_hop(way, c, relay(h, way, slot, c))

            pl.when(cond & inner if c == last_chunk else cond)(go)

    def relays_sent(to_ends):
        for h in range(1, rows):
            for cond, slot, way in ways(h):
                goes = to_end[way] if to_ends else exists[way] & jnp.logical_not(to_end[way])
                top = last_chunk if to_ends else len(chunks)
                for c in range(max(top - WINDOW, 0), top):
                    pl.when(cond & goes)(relay(h, way, slot, c).wait_send)

    def hops_done():
        relays_sent(False)
        for way in (UP, DOWN):
            for end, part in ((False, own), (True, own.at[:, pl.ds(0, early)])):
                goes = to_end[way] if end else exists[way] & jnp.logical_not(to_end[way])
                pl.when(goes)(remote(way, part, part, hop_send.at[way], hop_send.at[way]).wait_send)

    sides = ((0, r == 1, r == 0, UP, DOWN, CROSS_DOWN),
             (1, r == rows - 2, r == rows - 1, DOWN, UP, CROSS_UP))

    def pair_copy(side, way):
        return remote(way, facts_hbm, end_arrived.at[side], pair_sem.at[0], pair_sem.at[1 + side])

    def send_pairs():
        for side, _, end, way, _, _ in sides:
            pl.when(end)(pair_copy(side, way).start)

    def take_pairs():
        for side, serves, end, way, _, _ in sides:
            def take(side=side, way=way):
                pair_copy(side, way).wait_recv()
                keep = pltpu.make_async_copy(end_arrived.at[side], end_pairs.at[side], pair_sem.at[3])
                keep.start()
                keep.wait()

            pl.when(end)(pair_copy(side, way).wait_send)
            pl.when(serves)(take)

    def end_copy(side, far, way):
        return remote(way, end_stage.at[side, far],
                      col_pick.at[:, pl.ds(far * groups, groups), pl.ds(early, bins - early)],
                      end_send.at[side, far], end_recv.at[far])

    def serve_ends():
        for side, serves, _, _, near, cross_way in sides:
            def serve(side=side, near=near, cross_way=cross_way):
                for far, half, way in ((1, other, cross_way), (0, w, near)):
                    for t in range(owned):
                        j = end_pairs[side, 1, half * owned + t]
                        end_stage[side, far, t] = col[last_chunk][j]
                    end_copy(side, far, way).start()

            pl.when(serves)(serve)

    def ends_done():
        for side, serves, end, _, near, cross_way in sides:
            for far, way in ((1, cross_way), (0, near)):
                copy = end_copy(side, far, way)
                pl.when(serves)(copy.wait_send)
                pl.when(end)(copy.wait_recv)

    def pick_copy(part):
        return remote(PARTNER, stage.at[1, :, :, part], col_pick.at[:, pl.ds(groups, groups), part],
                      pick_sem.at[0], pick_sem.at[1])

    def pick_keep(part):
        return pltpu.make_async_copy(
            stage.at[0, :, :, part], col_pick.at[:, pl.ds(0, groups), part], pick_sem.at[2])

    def pick(c):
        if c == last_chunk:
            relays_sent(True)
            serve_ends()
            pl.when(inner)(lambda: pick_chunk(c))
        else:
            pick_chunk(c)

    def pick_chunk(c):
        k, n = chunks[c]
        for side, half in ((1, other), (0, w)):
            for t in range(owned):
                j = facts[1, half * owned + t]
                stage[side, t, :, k:k + n] = col[c][j]
            (pick_copy if side else pick_keep)(pl.ds(k, n)).start()

    get_facts.wait()
    fill_table(facts, kcol, table, rec.shape[2])
    ahead, both = min(AHEAD, last_chunk), min(BOTH, last_chunk)
    for g in range(groups):
        for i in range(g * GROUP // FETCH, (g + 1) * GROUP // FETCH):
            fetch(i).wait()
            for v in range(i * FETCH, (i + 1) * FETCH):
                s = lax.dot_general(table[...], rec[v], (((1,), (1,)), ((), ())),
                                    preferred_element_type=jnp.float32)
                scale = 1.0 / jnp.sqrt(jnp.mean(s * s, axis=0, keepdims=True) + 1e-06)
                s = s * scale
                first = v % GROUP
                for lane in range(spec.shape[0]):
                    part = s[:, lane * 128:(lane + 1) * 128]
                    spec[lane, pl.ds(first, bins, stride=2 * GROUP), :] = part[:bins]
                    spec[lane, pl.ds(first + GROUP, bins, stride=2 * GROUP), :] = part[bins:]
        for lane in range(spec.shape[0]):
            part = spec[lane].astype(jnp.bfloat16).reshape(bins, 2 * GROUP, 128)
            own[g, :, :, lane * 128:(lane + 1) * 128] = part
            for c, (k, n) in enumerate(chunks):
                col[c][r, g, :, :, lane * 128:(lane + 1) * 128] = part[k:k + n]
        if g == 0:
            pl.semaphore_wait(barrier, 2 + ends)
            send_pairs()
        for c in range(2):
            send_own(c, g, False)
            send_own(c, g, True)
        to_partner(g).start()
        for way in (RIGHT, LEFT, SIBLING):
            start(way, row_copy(way, own.at[g], q, g))
        for c in range(2, ahead if g == 0 else both):
            send_own(c, g, True)
    keep = pltpu.make_async_copy(own, row_set.at[q, pl.ds(0, groups)], local_sem.at[0])
    keep.start()

    last = len(chunks) + rows - 2
    row_work = {}
    for g in range(groups):
        row_work[2 + 2 * g] = lambda g=g: from_partner(g)
        row_work[3 + 2 * g] = lambda g=g: along_x(g)
        row_work[3 + 2 * groups + g] = lambda g=g: along_x(groups + g)
    for step in range(max(last, 3 + 3 * groups)):
        c = 2 + step
        if c < len(chunks):
            send_own(c, None, False)
        if both <= c < ahead:
            for g in range(1, groups):
                send_own(c, g, True)
        elif ahead <= c < last_chunk:
            send_own(c, None, True)
        for h in range(1, rows):
            if 0 <= step - h + 1 < len(chunks):
                hop(h, step - h + 1)
        if 0 <= step - rows + 2 < len(chunks):
            pick(step - rows + 2)
        if step == 1:
            take_pairs()
        if step in row_work:
            row_work[step]()

    rows_done()
    hops_done()
    for n, goes in ((bins, inner), (early, jnp.logical_not(inner))):
        def picks_done(n=n):
            pick_copy(pl.ds(0, n)).wait()
            pick_keep(pl.ds(0, n)).wait()

        pl.when(goes)(picks_done)
    ends_done()
    keep.wait()


def gather(records, facts, bins, rows, cols, owned):
    windows, channels, length = records.shape
    groups = windows // GROUP
    chunks = chunk_list(bins)
    count = len(chunks)
    hbm = pl.BlockSpec(memory_space=pl.ANY)
    dma = pltpu.SemaphoreType.DMA
    tile = (2 * GROUP, channels)
    return pl.pallas_call(
        functools.partial(gather_kernel, rows, cols, chunks),
        out_shape=(
            jax.ShapeDtypeStruct((cols, 2 * groups, bins) + tile, jnp.bfloat16),
            jax.ShapeDtypeStruct((owned, 2 * groups, bins) + tile, jnp.bfloat16)),
        in_specs=[hbm, hbm],
        out_specs=(hbm, hbm),
        scratch_shapes=[
            pltpu.SMEM(facts.shape, jnp.int32),
            dma((1,)),
            pltpu.VMEM((bins, 128), jnp.int32),
            pltpu.VMEM((2 * bins, length), jnp.bfloat16),
            pltpu.VMEM(records.shape, jnp.bfloat16),
            pltpu.VMEM((channels // 128, 2 * bins * GROUP, 128), jnp.float32),
            pltpu.VMEM((groups, bins) + tile, jnp.bfloat16),
            pltpu.VMEM((2, owned, groups, bins) + tile, jnp.bfloat16),
            pltpu.VMEM((2, 2, owned, groups, chunks[-1][1]) + tile, jnp.bfloat16),
            pltpu.VMEM((2,) + facts.shape, jnp.int32),
            pltpu.SMEM((2,) + facts.shape, jnp.int32),
            *[pltpu.VMEM((rows, groups, n) + tile, jnp.bfloat16) for _, n in chunks],
            dma((windows // FETCH,)),
            dma((1,)),
            dma((1,)),
            dma((3, cols)),
            dma((cols // 2, 2 * groups)),
            dma((cols // 2,)),
            dma((2,)),
            dma((2, rows - 1, WINDOW)),
            dma((rows - 1, count)),
            dma((3,)),
            dma((4,)),
            dma((2, 2)),
            dma((2,)),
        ],
        compiler_params=pltpu.CompilerParams(
            collective_id=0, has_side_effects=True, vmem_limit_bytes=40 * 2**20),
        cost_estimate=pl.CostEstimate(
            flops=4 * windows * channels * length * bins,
            bytes_accessed=windows * channels * length * 2, transcendentals=0),
    )(facts, records)


def cross_kernel(owned, facts, row_set, col_pick, out, ring, sem):
    depth, _, step, channels, _ = ring.shape
    groups = row_set.shape[1]
    chunks = out.shape[4] // step

    def copy(n):
        part = pl.ds((n % chunks) * step, step)
        return pltpu.make_async_copy(
            ring.at[n % depth], out.at[0, 0, n // chunks, :, part], sem.at[n % depth])

    def one(n, _):
        slot = n % depth
        position = lax.axis_index("win") * owned + n // chunks
        i = facts[0, position]
        live = position < facts[3, 0]

        @pl.when(n >= depth)
        def _():
            copy(n - depth).wait()

        @pl.when(live)
        def _():
            for t in range(step):
                k = (n % chunks) * step + t
                a = row_set[i, :, k].reshape(-1, channels)
                b = col_pick[n // chunks, :, k].reshape(a.shape)
                parts = b.astype(jnp.float32).reshape(groups, 2, GROUP, channels)
                turned = jnp.concatenate([-parts[:, 1:], parts[:, :1]], axis=1)
                turned = turned.reshape(a.shape).astype(jnp.bfloat16)
                both = lax.dot_general(
                    a, jnp.concatenate([b, turned], axis=1), (((0,), (0,)), ((), ())),
                    preferred_element_type=jnp.float32)
                ring[slot, 0, t] = both[:, :channels].astype(jnp.bfloat16)
                ring[slot, 1, t] = both[:, channels:].astype(jnp.bfloat16)

        @pl.when(jnp.logical_not(live))
        def _():
            ring[slot] = jnp.zeros(ring.shape[1:], jnp.bfloat16)

        copy(n).start()
        return 0

    total = owned * chunks
    lax.fori_loop(0, total, one, 0)
    for n in range(max(total - depth, 0), total):
        copy(n).wait()


def cross(row_set, col_pick, facts):
    owned, groups, bins, entries, channels = col_pick.shape
    step = math.gcd(bins, 8)
    smem = pl.BlockSpec(memory_space=pltpu.SMEM)
    vmem = pl.BlockSpec(memory_space=pltpu.VMEM)
    return pl.pallas_call(
        functools.partial(cross_kernel, owned),
        out_shape=jax.ShapeDtypeStruct(
            (1, 1, owned, 2, bins, channels, channels), jnp.bfloat16),
        in_specs=[smem, vmem, vmem],
        out_specs=pl.BlockSpec(memory_space=pl.ANY),
        scratch_shapes=[
            pltpu.VMEM((4, 2, step, channels, channels), jnp.bfloat16),
            pltpu.SemaphoreType.DMA((4,)),
        ],
        compiler_params=pltpu.CompilerParams(vmem_limit_bytes=40 * 2**20),
        cost_estimate=pl.CostEstimate(
            flops=4 * owned * bins * channels * channels * groups * entries,
            bytes_accessed=4 * owned * bins * channels * channels, transcendentals=0),
    )(facts, row_set, col_pick)


def body(records, tile_pairs, tile_count, bin_index):
    rows, cols = lax.axis_size("row"), lax.axis_size("col")
    owned = tile_pairs.shape[2] // lax.axis_size("win")
    slots, bins = tile_pairs.shape[2], bin_index.shape[0]
    facts = (jnp.pad(jnp.swapaxes(tile_pairs, 2, 3).reshape(2, slots), ((0, 2), (0, 128 - slots)))
             + jnp.pad(bin_index.reshape(1, bins), ((2, 1), (0, 128 - bins)))
             + jnp.pad(tile_count.reshape(1, 1), ((3, 0), (0, 127))))
    row_set, col_pick = gather(records, facts, bins, rows, cols, owned)
    return cross(row_set, col_pick, facts)


def solution(mesh):
    return jax.shard_map(
        body,
        mesh=mesh,
        in_specs=(
            P("win", ("row", "col"), None),
            P("row", "col", None, None),
            P("row", "col"),
            P(),
        ),
        out_specs=P("row", "col", "win", None, None, None, None),
        check_vma=False,
    )
```

```python
import functools
import math

import jax
import jax.numpy as jnp
from jax import lax
from jax.experimental import pallas as pl
from jax.experimental.pallas import tpu as pltpu
from jax.sharding import PartitionSpec as P

GROUP = 8
FETCH = 4
AHEAD = 5
BOTH = 3
WINDOW = 2
UP, DOWN, PARTNER, RIGHT, LEFT, SIBLING, CROSS_UP, CROSS_DOWN = range(8)


def chunk_list(bins):
    size = max(bins // 8, 1)
    starts = list(range(0, 6 * size, size))
    if size > 3:
        starts += [6 * size - size // 2, 6 * size + size // 4]
    return [(a, b - a) for a, b in zip(starts, starts[1:] + [bins])]


def cos_sin(phase, length):
    shift = length.bit_length() - 3
    turn = (phase + (1 << shift >> 1)) >> shift
    x = (phase - (turn << shift)).astype(jnp.float32) * (2.0 * math.pi / length)
    y = x * x
    c = 1.0 + y * (-0.5 + y * (1.0 / 24 + y * (-1.0 / 720 + y * (1.0 / 40320))))
    s = x * (1.0 + y * (-1.0 / 6 + y * (1.0 / 120 + y * (-1.0 / 5040 + y * (1.0 / 362880)))))
    odd = (turn & 1) == 1
    cosine, sine = jnp.where(odd, s, c), jnp.where(odd, c, s)
    cosine = jnp.where(((turn + 1) & 2) == 2, -cosine, cosine)
    sine = jnp.where((turn & 2) == 2, -sine, sine)
    return cosine, sine


def fill_table(facts, kcol, table, length):
    assert length & (length - 1) == 0
    bins = kcol.shape[0]
    for k in range(bins):
        kcol[k:k + 1, :] = jnp.full((1, 128), facts[2, k], jnp.int32)
    for lane in range(0, length, 128):
        samples = lax.broadcasted_iota(jnp.int32, (8, 128), 1) + lane
        taper = 0.5 - 0.5 * cos_sin(samples, length)[0]
        taper = jnp.concatenate([taper] * (bins // 8), axis=0)
        samples = jnp.concatenate([samples] * (bins // 8), axis=0)
        cosine, sine = cos_sin(kcol[...] * samples & (length - 1), length)
        table[:bins, lane:lane + 128] = (taper * cosine).astype(jnp.bfloat16)
        table[bins:, lane:lane + 128] = (-taper * sine).astype(jnp.bfloat16)


def gather_kernel(rows, cols, chunks, facts_hbm, rec_hbm, row_set, col_pick,
                  facts, facts_sem, kcol, table, rec, spec, own, stage,
                  end_stage, end_arrived, end_pairs, *rest):
    col = rest[:len(chunks)]
    (rec_sem, local_sem, partner_send, row_send, row_recv, sibling_recv, hop_send, relay_send, hop_recv,
     pick_sem, pair_sem, end_send, end_recv) = rest[len(chunks):]
    groups, bins = own.shape[0], own.shape[1]
    owned = stage.shape[1]
    w, r, q = lax.axis_index("win"), lax.axis_index("row"), lax.axis_index("col")
    chips = cols // 2
    x = q // 2
    other = 1 - w
    device = {
        UP: (w, r + 1, q), DOWN: (w, r - 1, q), PARTNER: (other, r, q),
        RIGHT: (w, r, q + 2), LEFT: (w, r, q - 2), SIBLING: (w, r, q + 1 - 2 * (q % 2)),
        CROSS_UP: (other, r + 1, q), CROSS_DOWN: (other, r - 1, q),
    }
    exists = {
        UP: r < rows - 1, DOWN: r > 0, PARTNER: None,
        RIGHT: x < chips - 1, LEFT: x > 0, SIBLING: None,
        CROSS_UP: (r == 0) | (r == rows - 2), CROSS_DOWN: (r == 1) | (r == rows - 1),
    }

    last_chunk = len(chunks) - 1
    early = chunks[last_chunk][0]
    inner = (r > 0) & (r < rows - 1)
    to_end = {UP: r == rows - 2, DOWN: r == 1}

    def fetch(i):
        part = pl.ds(i * FETCH, FETCH)
        return pltpu.make_async_copy(rec_hbm.at[part], rec.at[part], rec_sem.at[i])

    get_facts = pltpu.make_async_copy(facts_hbm, facts, facts_sem.at[0])
    get_facts.start()
    for i in range(groups * GROUP // FETCH):
        fetch(i).start()

    def guarded(way, f):
        if exists[way] is None:
            f()
        else:
            pl.when(exists[way])(f)

    barrier = pltpu.get_barrier_semaphore()
    for way in range(8):
        guarded(way, lambda way=way: pl.semaphore_signal(
            barrier, inc=1, device_id=device[way], device_id_type=pl.DeviceIdType.MESH))
    ends = sum(exists[way].astype(jnp.int32)
               for way in (UP, DOWN, RIGHT, LEFT, CROSS_UP, CROSS_DOWN))

    def remote(way, src, dst, send_sem, recv_sem):
        return pltpu.make_async_remote_copy(
            src_ref=src, dst_ref=dst, send_sem=send_sem, recv_sem=recv_sem,
            device_id=device[way], device_id_type=pl.DeviceIdType.MESH)

    def start(way, copy):
        guarded(way, copy.start)

    def row_copy(way, src, slot, part):
        recv = sibling_recv.at[slot // 2] if way == SIBLING else row_recv.at[slot // 2, part]
        return remote(way, src, row_set.at[slot, part], row_send.at[way - RIGHT, slot], recv)

    def row_arrived(slot, part):
        row_copy(RIGHT, row_set.at[slot, part], slot, part).wait_recv()

    def row_relay(cond, slot, part, ways):
        def go():
            row_arrived(slot, part)
            for way in ways:
                start(way, row_copy(way, row_set.at[slot, part], slot, part))

        pl.when(cond)(go)

    def along_x(part):
        for d in range(1, chips):
            row_relay(x - d >= 0, q - 2 * d, part, (RIGHT, SIBLING))
            row_relay(x + d < chips, q + 2 * d, part, (LEFT, SIBLING))

    def to_partner(g):
        return remote(PARTNER, own.at[g], row_set.at[q, groups + g],
                      partner_send.at[0], row_recv.at[q // 2, groups + g])

    def from_partner(g):
        part = groups + g
        row_arrived(q, part)
        for way in (RIGHT, LEFT, SIBLING):
            start(way, row_copy(way, row_set.at[q, part], q, part))

    def rows_done():
        def slot_bytes(way, slot):
            return remote(way, row_set.at[slot], row_set.at[slot],
                          row_send.at[way - RIGHT, slot], sibling_recv.at[slot // 2])

        remote(PARTNER, own, own, partner_send.at[0], partner_send.at[0]).wait_send()
        for way in (RIGHT, LEFT, SIBLING):
            guarded(way, slot_bytes(way, q).wait_send)
        for d in range(1, chips):
            for cond, slot, way in ((x - d >= 0, q - 2 * d, RIGHT), (x + d < chips, q + 2 * d, LEFT)):
                def done(slot=slot, way=way):
                    guarded(way, slot_bytes(way, slot).wait_send)
                    slot_bytes(SIBLING, slot).wait_send()

                pl.when(cond)(done)
        for c in range(chips):
            slot_bytes(SIBLING, 2 * c + 1 - q % 2).wait_recv()

    def hop_copy(way, slot, c, src, dst, sem):
        return remote(way, src, dst, sem, hop_recv.at[slot - (1 if way == DOWN else 0), c])

    def start_hop(way, c, copy, wait=False):
        goes = exists[way]
        if c == last_chunk:
            goes = goes & jnp.logical_not(to_end[way])
        pl.when(goes)(copy.wait_send if wait else copy.start)

    def send_own(c, g, to_ends):
        k, n = chunks[c]
        for way in (UP, DOWN):
            goes = to_end[way] if to_ends else exists[way] & jnp.logical_not(to_end[way])
            if g is None:
                copy = hop_copy(way, r, c, own.at[:, pl.ds(k, n)], col[c].at[r], hop_send.at[way])
            else:
                copy = hop_copy(way, r, c, own.at[g, pl.ds(k, n)], col[c].at[r, g],
                                hop_send.at[way])
            pl.when(goes)(copy.start)

    def relay(h, way, slot, c):
        return hop_copy(way, slot, c, col[c].at[slot], col[c].at[slot],
                        relay_send.at[way, h - 1, c % WINDOW])

    def ways(h):
        return (r - h >= 0, r - h, UP), (r + h < rows, r + h, DOWN)

    def hop(h, c):
        for cond, slot, way in ways(h):
            def go(slot=slot, way=way):
                relay(h, way, slot, c).wait_recv()
                if c >= WINDOW:
                    start_hop(way, c, relay(h, way, slot, c - WINDOW), True)
                start_hop(way, c, relay(h, way, slot, c))

            pl.when(cond & inner if c == last_chunk else cond)(go)

    def relays_sent(to_ends):
        for h in range(1, rows):
            for cond, slot, way in ways(h):
                goes = to_end[way] if to_ends else exists[way] & jnp.logical_not(to_end[way])
                top = last_chunk if to_ends else len(chunks)
                for c in range(max(top - WINDOW, 0), top):
                    pl.when(cond & goes)(relay(h, way, slot, c).wait_send)

    def hops_done():
        relays_sent(False)
        for way in (UP, DOWN):
            for end, part in ((False, own), (True, own.at[:, pl.ds(0, early)])):
                goes = to_end[way] if end else exists[way] & jnp.logical_not(to_end[way])
                pl.when(goes)(remote(way, part, part, hop_send.at[way], hop_send.at[way]).wait_send)

    sides = ((0, r == 1, r == 0, UP, DOWN, CROSS_DOWN),
             (1, r == rows - 2, r == rows - 1, DOWN, UP, CROSS_UP))

    def pair_copy(side, way):
        return remote(way, facts_hbm, end_arrived.at[side], pair_sem.at[0], pair_sem.at[1 + side])

    def send_pairs():
        for side, _, end, way, _, _ in sides:
            pl.when(end)(pair_copy(side, way).start)

    def take_pairs():
        for side, serves, end, way, _, _ in sides:
            def take(side=side, way=way):
                pair_copy(side, way).wait_recv()
                keep = pltpu.make_async_copy(end_arrived.at[side], end_pairs.at[side], pair_sem.at[3])
                keep.start()
                keep.wait()

            pl.when(end)(pair_copy(side, way).wait_send)
            pl.when(serves)(take)

    def end_copy(side, far, way):
        return remote(way, end_stage.at[side, far],
                      col_pick.at[:, pl.ds(far * groups, groups), pl.ds(early, bins - early)],
                      end_send.at[side, far], end_recv.at[far])

    def serve_ends():
        for side, serves, _, _, near, cross_way in sides:
            def serve(side=side, near=near, cross_way=cross_way):
                for far, half, way in ((1, other, cross_way), (0, w, near)):
                    for t in range(owned):
                        j = end_pairs[side, 1, half * owned + t]
                        end_stage[side, far, t] = col[last_chunk][j]
                    end_copy(side, far, way).start()

            pl.when(serves)(serve)

    def ends_done():
        for side, serves, end, _, near, cross_way in sides:
            for far, way in ((1, cross_way), (0, near)):
                copy = end_copy(side, far, way)
                pl.when(serves)(copy.wait_send)
                pl.when(end)(copy.wait_recv)

    def pick_copy(part):
        return remote(PARTNER, stage.at[1, :, :, part], col_pick.at[:, pl.ds(groups, groups), part],
                      pick_sem.at[0], pick_sem.at[1])

    def pick_keep(part):
        return pltpu.make_async_copy(
            stage.at[0, :, :, part], col_pick.at[:, pl.ds(0, groups), part], pick_sem.at[2])

    def pick(c):
        if c == last_chunk:
            relays_sent(True)
            serve_ends()
            pl.when(inner)(lambda: pick_chunk(c))
        else:
            pick_chunk(c)

    def pick_chunk(c):
        k, n = chunks[c]
        for side, half in ((1, other), (0, w)):
            for t in range(owned):
                j = facts[1, half * owned + t]
                stage[side, t, :, k:k + n] = col[c][j]
            (pick_copy if side else pick_keep)(pl.ds(k, n)).start()

    get_facts.wait()
    fill_table(facts, kcol, table, rec.shape[2])
    ahead, both = min(AHEAD, last_chunk), min(BOTH, last_chunk)
    for g in range(groups):
        for i in range(g * GROUP // FETCH, (g + 1) * GROUP // FETCH):
            fetch(i).wait()
            for v in range(i * FETCH, (i + 1) * FETCH):
                s = lax.dot_general(table[...], rec[v], (((1,), (1,)), ((), ())),
                                    preferred_element_type=jnp.float32)
                scale = 1.0 / jnp.sqrt(jnp.mean(s * s, axis=0, keepdims=True) + 1e-06)
                s = s * scale
                first = v % GROUP
                for lane in range(spec.shape[0]):
                    part = s[:, lane * 128:(lane + 1) * 128]
                    spec[lane, pl.ds(first, bins, stride=2 * GROUP), :] = part[:bins]
                    spec[lane, pl.ds(first + GROUP, bins, stride=2 * GROUP), :] = part[bins:]
        for lane in range(spec.shape[0]):
            part = spec[lane].astype(jnp.bfloat16).reshape(bins, 2 * GROUP, 128)
            own[g, :, :, lane * 128:(lane + 1) * 128] = part
            for c, (k, n) in enumerate(chunks):
                col[c][r, g, :, :, lane * 128:(lane + 1) * 128] = part[k:k + n]
        if g == 0:
            pl.semaphore_wait(barrier, 2 + ends)
            send_pairs()
        for c in range(2):
            send_own(c, g, False)
            send_own(c, g, True)
        to_partner(g).start()
        for way in (RIGHT, LEFT, SIBLING):
            start(way, row_copy(way, own.at[g], q, g))
        for c in range(2, ahead if g == 0 else both):
            send_own(c, g, True)
    keep = pltpu.make_async_copy(own, row_set.at[q, pl.ds(0, groups)], local_sem.at[0])
    keep.start()

    last = len(chunks) + rows - 2
    row_work = {}
    for g in range(groups):
        row_work[2 + 2 * g] = lambda g=g: from_partner(g)
        row_work[3 + 2 * g] = lambda g=g: along_x(g)
        row_work[3 + 2 * groups + g] = lambda g=g: along_x(groups + g)
    for step in range(max(last, 3 + 3 * groups)):
        c = 2 + step
        if c < len(chunks):
            send_own(c, None, False)
        if both <= c < ahead:
            for g in range(1, groups):
                send_own(c, g, True)
        elif ahead <= c < last_chunk:
            send_own(c, None, True)
        for h in range(1, rows):
            if 0 <= step - h + 1 < len(chunks):
                hop(h, step - h + 1)
        if 0 <= step - rows + 2 < len(chunks):
            pick(step - rows + 2)
        if step == 1:
            take_pairs()
        if step in row_work:
            row_work[step]()

    rows_done()
    hops_done()
    for n, goes in ((bins, inner), (early, jnp.logical_not(inner))):
        def picks_done(n=n):
            pick_copy(pl.ds(0, n)).wait()
            pick_keep(pl.ds(0, n)).wait()

        pl.when(goes)(picks_done)
    ends_done()
    keep.wait()


def gather(records, facts, bins, rows, cols, owned):
    windows, channels, length = records.shape
    groups = windows // GROUP
    chunks = chunk_list(bins)
    count = len(chunks)
    hbm = pl.BlockSpec(memory_space=pl.ANY)
    dma = pltpu.SemaphoreType.DMA
    tile = (2 * GROUP, channels)
    return pl.pallas_call(
        functools.partial(gather_kernel, rows, cols, chunks),
        out_shape=(
            jax.ShapeDtypeStruct((cols, 2 * groups, bins) + tile, jnp.bfloat16),
            jax.ShapeDtypeStruct((owned, 2 * groups, bins) + tile, jnp.bfloat16)),
        in_specs=[hbm, hbm],
        out_specs=(hbm, hbm),
        scratch_shapes=[
            pltpu.SMEM(facts.shape, jnp.int32),
            dma((1,)),
            pltpu.VMEM((bins, 128), jnp.int32),
            pltpu.VMEM((2 * bins, length), jnp.bfloat16),
            pltpu.VMEM(records.shape, jnp.bfloat16),
            pltpu.VMEM((channels // 128, 2 * bins * GROUP, 128), jnp.float32),
            pltpu.VMEM((groups, bins) + tile, jnp.bfloat16),
            pltpu.VMEM((2, owned, groups, bins) + tile, jnp.bfloat16),
            pltpu.VMEM((2, 2, owned, groups, chunks[-1][1]) + tile, jnp.bfloat16),
            pltpu.VMEM((2,) + facts.shape, jnp.int32),
            pltpu.SMEM((2,) + facts.shape, jnp.int32),
            *[pltpu.VMEM((rows, groups, n) + tile, jnp.bfloat16) for _, n in chunks],
            dma((windows // FETCH,)),
            dma((1,)),
            dma((1,)),
            dma((3, cols)),
            dma((cols // 2, 2 * groups)),
            dma((cols // 2,)),
            dma((2,)),
            dma((2, rows - 1, WINDOW)),
            dma((rows - 1, count)),
            dma((3,)),
            dma((4,)),
            dma((2, 2)),
            dma((2,)),
        ],
        compiler_params=pltpu.CompilerParams(
            collective_id=0, has_side_effects=True, vmem_limit_bytes=40 * 2**20),
        cost_estimate=pl.CostEstimate(
            flops=4 * windows * channels * length * bins,
            bytes_accessed=windows * channels * length * 2, transcendentals=0),
    )(facts, records)


def cross_kernel(owned, facts, row_set, col_pick, out, ring, sem):
    depth, _, step, channels, _ = ring.shape
    groups = row_set.shape[1]
    chunks = out.shape[4] // step
    piece = step // sem.shape[1]

    def copy(n, p):
        return pltpu.make_async_copy(
            ring.at[n % depth, :, pl.ds(p * piece, piece)],
            out.at[0, 0, n // chunks, :, pl.ds((n % chunks) * step + p * piece, piece)],
            sem.at[n % depth, p])

    pieces = range(sem.shape[1])

    def one(n, _):
        slot = n % depth
        position = lax.axis_index("win") * owned + n // chunks
        i = facts[0, position]
        live = position < facts[3, 0]

        @pl.when(n >= depth)
        def _():
            for p in pieces:
                copy(n - depth, p).wait()

        @pl.when(live)
        def _():
            for p in pieces:
                for t in range(p * piece, (p + 1) * piece):
                    k = (n % chunks) * step + t
                    a = row_set[i, :, k].reshape(-1, channels)
                    b = col_pick[n // chunks, :, k].reshape(a.shape)
                    parts = b.astype(jnp.float32).reshape(groups, 2, GROUP, channels)
                    turned = jnp.concatenate([-parts[:, 1:], parts[:, :1]], axis=1)
                    turned = turned.reshape(a.shape).astype(jnp.bfloat16)
                    both = lax.dot_general(
                        a, jnp.concatenate([b, turned], axis=1), (((0,), (0,)), ((), ())),
                        preferred_element_type=jnp.float32)
                    ring[slot, 0, t] = both[:, :channels].astype(jnp.bfloat16)
                    ring[slot, 1, t] = both[:, channels:].astype(jnp.bfloat16)
                copy(n, p).start()

        @pl.when(jnp.logical_not(live))
        def _():
            ring[slot] = jnp.zeros(ring.shape[1:], jnp.bfloat16)
            for p in pieces:
                copy(n, p).start()

        return 0

    total = owned * chunks
    lax.fori_loop(0, total, one, 0)
    for n in range(max(total - depth, 0), total):
        for p in pieces:
            copy(n, p).wait()


def cross(row_set, col_pick, facts):
    owned, groups, bins, entries, channels = col_pick.shape
    step = math.gcd(bins, 16)
    piece = math.gcd(step, 4)
    smem = pl.BlockSpec(memory_space=pltpu.SMEM)
    vmem = pl.BlockSpec(memory_space=pltpu.VMEM)
    return pl.pallas_call(
        functools.partial(cross_kernel, owned),
        out_shape=jax.ShapeDtypeStruct(
            (1, 1, owned, 2, bins, channels, channels), jnp.bfloat16),
        in_specs=[smem, vmem, vmem],
        out_specs=pl.BlockSpec(memory_space=pl.ANY),
        scratch_shapes=[
            pltpu.VMEM((2, 2, step, channels, channels), jnp.bfloat16),
            pltpu.SemaphoreType.DMA((2, step // piece)),
        ],
        compiler_params=pltpu.CompilerParams(vmem_limit_bytes=40 * 2**20),
        cost_estimate=pl.CostEstimate(
            flops=4 * owned * bins * channels * channels * groups * entries,
            bytes_accessed=4 * owned * bins * channels * channels, transcendentals=0),
    )(facts, row_set, col_pick)


def body(records, tile_pairs, tile_count, bin_index):
    rows, cols = lax.axis_size("row"), lax.axis_size("col")
    owned = tile_pairs.shape[2] // lax.axis_size("win")
    slots, bins = tile_pairs.shape[2], bin_index.shape[0]
    facts = (jnp.pad(jnp.swapaxes(tile_pairs, 2, 3).reshape(2, slots), ((0, 2), (0, 128 - slots)))
             + jnp.pad(bin_index.reshape(1, bins), ((2, 1), (0, 128 - bins)))
             + jnp.pad(tile_count.reshape(1, 1), ((3, 0), (0, 127))))
    row_set, col_pick = gather(records, facts, bins, rows, cols, owned)
    return cross(row_set, col_pick, facts)


def solution(mesh):
    return jax.shard_map(
        body,
        mesh=mesh,
        in_specs=(
            P("win", ("row", "col"), None),
            P("row", "col", None, None),
            P("row", "col"),
            P(),
        ),
        out_specs=P("row", "col", "win", None, None, None, None),
        check_vma=False,
    )
```

```python
import functools
import math

import jax
import jax.numpy as jnp
from jax import lax
from jax.experimental import pallas as pl
from jax.experimental.pallas import tpu as pltpu
from jax.sharding import PartitionSpec as P

GROUP = 8
FETCH = 4
AHEAD = 5
BOTH = 3
WINDOW = 2
UP, DOWN, PARTNER, RIGHT, LEFT, SIBLING, CROSS_UP, CROSS_DOWN = range(8)


def chunk_list(bins):
    size = max(bins // 8, 1)
    starts = list(range(0, 6 * size, size))
    if size > 3:
        starts += [6 * size - size // 2, 6 * size + size // 4]
    return [(a, b - a) for a, b in zip(starts, starts[1:] + [bins])]


def cos_sin(phase, length):
    shift = length.bit_length() - 3
    turn = (phase + (1 << shift >> 1)) >> shift
    x = (phase - (turn << shift)).astype(jnp.float32) * (2.0 * math.pi / length)
    y = x * x
    c = 1.0 + y * (-0.5 + y * (1.0 / 24 + y * (-1.0 / 720 + y * (1.0 / 40320))))
    s = x * (1.0 + y * (-1.0 / 6 + y * (1.0 / 120 + y * (-1.0 / 5040 + y * (1.0 / 362880)))))
    odd = (turn & 1) == 1
    cosine, sine = jnp.where(odd, s, c), jnp.where(odd, c, s)
    cosine = jnp.where(((turn + 1) & 2) == 2, -cosine, cosine)
    sine = jnp.where((turn & 2) == 2, -sine, sine)
    return cosine, sine


def fill_table(facts, kcol, table, length):
    assert length & (length - 1) == 0
    bins = kcol.shape[0]
    for k in range(bins):
        kcol[k:k + 1, :] = jnp.full((1, 128), facts[2, k], jnp.int32)
    for lane in range(0, length, 128):
        samples = lax.broadcasted_iota(jnp.int32, (8, 128), 1) + lane
        taper = 0.5 - 0.5 * cos_sin(samples, length)[0]
        taper = jnp.concatenate([taper] * (bins // 8), axis=0)
        samples = jnp.concatenate([samples] * (bins // 8), axis=0)
        cosine, sine = cos_sin(kcol[...] * samples & (length - 1), length)
        table[:bins, lane:lane + 128] = (taper * cosine).astype(jnp.bfloat16)
        table[bins:, lane:lane + 128] = (-taper * sine).astype(jnp.bfloat16)


def gather_kernel(rows, cols, chunks, facts_hbm, rec_hbm, row_set, col_pick,
                  facts, facts_sem, kcol, table, rec, spec, own, stage,
                  end_stage, end_arrived, end_pairs, *rest):
    col = rest[:len(chunks)]
    (rec_sem, local_sem, partner_send, row_send, row_recv, sibling_recv, hop_send, relay_send, hop_recv,
     pick_sem, pair_sem, end_send, end_recv) = rest[len(chunks):]
    groups, bins = own.shape[0], own.shape[1]
    owned = stage.shape[1]
    w, r, q = lax.axis_index("win"), lax.axis_index("row"), lax.axis_index("col")
    chips = cols // 2
    x = q // 2
    other = 1 - w
    device = {
        UP: (w, r + 1, q), DOWN: (w, r - 1, q), PARTNER: (other, r, q),
        RIGHT: (w, r, q + 2), LEFT: (w, r, q - 2), SIBLING: (w, r, q + 1 - 2 * (q % 2)),
        CROSS_UP: (other, r + 1, q), CROSS_DOWN: (other, r - 1, q),
    }
    exists = {
        UP: r < rows - 1, DOWN: r > 0, PARTNER: None,
        RIGHT: x < chips - 1, LEFT: x > 0, SIBLING: None,
        CROSS_UP: (r == 0) | (r == rows - 2), CROSS_DOWN: (r == 1) | (r == rows - 1),
    }

    last_chunk = len(chunks) - 1
    early = chunks[last_chunk][0]
    inner = (r > 0) & (r < rows - 1)
    to_end = {UP: r == rows - 2, DOWN: r == 1}

    halves = spec.shape[0]
    pieces = [(v, lane * 128, 128) for lane in range(halves) for v in range(0, GROUP, FETCH)]
    pieces += [(v, 0, halves * 128) for v in range(GROUP, groups * GROUP, FETCH)]

    def fetch(i):
        v, c, n = pieces[i]
        part = (pl.ds(v, FETCH), pl.ds(c, n))
        return pltpu.make_async_copy(rec_hbm.at[part], rec.at[part], rec_sem.at[i])

    get_facts = pltpu.make_async_copy(facts_hbm, facts, facts_sem.at[0])
    get_facts.start()
    for i in range(len(pieces)):
        fetch(i).start()

    def guarded(way, f):
        if exists[way] is None:
            f()
        else:
            pl.when(exists[way])(f)

    barrier = pltpu.get_barrier_semaphore()
    for way in range(8):
        guarded(way, lambda way=way: pl.semaphore_signal(
            barrier, inc=1, device_id=device[way], device_id_type=pl.DeviceIdType.MESH))
    ends = sum(exists[way].astype(jnp.int32)
               for way in (UP, DOWN, RIGHT, LEFT, CROSS_UP, CROSS_DOWN))

    def remote(way, src, dst, send_sem, recv_sem):
        return pltpu.make_async_remote_copy(
            src_ref=src, dst_ref=dst, send_sem=send_sem, recv_sem=recv_sem,
            device_id=device[way], device_id_type=pl.DeviceIdType.MESH)

    def start(way, copy):
        guarded(way, copy.start)

    def row_copy(way, src, slot, part):
        recv = sibling_recv.at[slot // 2] if way == SIBLING else row_recv.at[slot // 2, part]
        return remote(way, src, row_set.at[slot, part], row_send.at[way - RIGHT, slot], recv)

    def row_arrived(slot, part):
        row_copy(RIGHT, row_set.at[slot, part], slot, part).wait_recv()

    def row_relay(cond, slot, part, ways):
        def go():
            row_arrived(slot, part)
            for way in ways:
                start(way, row_copy(way, row_set.at[slot, part], slot, part))

        pl.when(cond)(go)

    def along_x(part):
        for d in range(1, chips):
            row_relay(x - d >= 0, q - 2 * d, part, (RIGHT, SIBLING))
            row_relay(x + d < chips, q + 2 * d, part, (LEFT, SIBLING))

    def to_partner(g):
        return remote(PARTNER, own.at[g], row_set.at[q, groups + g],
                      partner_send.at[0], row_recv.at[q // 2, groups + g])

    def from_partner(g):
        part = groups + g
        row_arrived(q, part)
        for way in (RIGHT, LEFT, SIBLING):
            start(way, row_copy(way, row_set.at[q, part], q, part))

    def rows_done():
        def slot_bytes(way, slot):
            return remote(way, row_set.at[slot], row_set.at[slot],
                          row_send.at[way - RIGHT, slot], sibling_recv.at[slot // 2])

        remote(PARTNER, own, own, partner_send.at[0], partner_send.at[0]).wait_send()
        for way in (RIGHT, LEFT, SIBLING):
            guarded(way, slot_bytes(way, q).wait_send)
        for d in range(1, chips):
            for cond, slot, way in ((x - d >= 0, q - 2 * d, RIGHT), (x + d < chips, q + 2 * d, LEFT)):
                def done(slot=slot, way=way):
                    guarded(way, slot_bytes(way, slot).wait_send)
                    slot_bytes(SIBLING, slot).wait_send()

                pl.when(cond)(done)
        for c in range(chips):
            slot_bytes(SIBLING, 2 * c + 1 - q % 2).wait_recv()

    def hop_copy(way, slot, c, src, dst, sem):
        return remote(way, src, dst, sem, hop_recv.at[slot - (1 if way == DOWN else 0), c])

    def start_hop(way, c, copy, wait=False):
        goes = exists[way]
        if c == last_chunk:
            goes = goes & jnp.logical_not(to_end[way])
        pl.when(goes)(copy.wait_send if wait else copy.start)

    def send_own(c, g, to_ends):
        k, n = chunks[c]
        for way in (UP, DOWN):
            goes = to_end[way] if to_ends else exists[way] & jnp.logical_not(to_end[way])
            if g is None:
                copy = hop_copy(way, r, c, own.at[:, pl.ds(k, n)], col[c].at[r], hop_send.at[way])
            else:
                copy = hop_copy(way, r, c, own.at[g, pl.ds(k, n)], col[c].at[r, g],
                                hop_send.at[way])
            pl.when(goes)(copy.start)

    def send_half(c, lane):
        part = (0, pl.ds(*chunks[c]), slice(None), pl.ds(lane * 128, 128))
        for way in (UP, DOWN):
            pl.when(to_end[way])(hop_copy(
                way, r, c, own.at[part], col[c].at[(r, 0) + (slice(None),) * 2 + part[3:]],
                hop_send.at[way]).start)

    def relay(h, way, slot, c):
        return hop_copy(way, slot, c, col[c].at[slot], col[c].at[slot],
                        relay_send.at[way, h - 1, c % WINDOW])

    def ways(h):
        return (r - h >= 0, r - h, UP), (r + h < rows, r + h, DOWN)

    def hop(h, c):
        for cond, slot, way in ways(h):
            def go(slot=slot, way=way):
                relay(h, way, slot, c).wait_recv()
                if c >= WINDOW:
                    start_hop(way, c, relay(h, way, slot, c - WINDOW), True)
                start_hop(way, c, relay(h, way, slot, c))

            pl.when(cond & inner if c == last_chunk else cond)(go)

    def relays_sent(to_ends):
        for h in range(1, rows):
            for cond, slot, way in ways(h):
                goes = to_end[way] if to_ends else exists[way] & jnp.logical_not(to_end[way])
                top = last_chunk if to_ends else len(chunks)
                for c in range(max(top - WINDOW, 0), top):
                    pl.when(cond & goes)(relay(h, way, slot, c).wait_send)

    def hops_done():
        relays_sent(False)
        for way in (UP, DOWN):
            for end, part in ((False, own), (True, own.at[:, pl.ds(0, early)])):
                goes = to_end[way] if end else exists[way] & jnp.logical_not(to_end[way])
                pl.when(goes)(remote(way, part, part, hop_send.at[way], hop_send.at[way]).wait_send)

    sides = ((0, r == 1, r == 0, UP, DOWN, CROSS_DOWN),
             (1, r == rows - 2, r == rows - 1, DOWN, UP, CROSS_UP))

    def pair_copy(side, way):
        return remote(way, facts_hbm, end_arrived.at[side], pair_sem.at[0], pair_sem.at[1 + side])

    def send_facts():
        for side, _, end, way, _, _ in sides:
            pl.when(end)(pair_copy(side, way).start)

    def take_pairs():
        for side, serves, end, way, _, _ in sides:
            def take(side=side, way=way):
                pair_copy(side, way).wait_recv()
                keep = pltpu.make_async_copy(end_arrived.at[side], end_pairs.at[side], pair_sem.at[3])
                keep.start()
                keep.wait()

            pl.when(end)(pair_copy(side, way).wait_send)
            pl.when(serves)(take)

    def end_copy(side, far, way):
        return remote(way, end_stage.at[side, far],
                      col_pick.at[:, pl.ds(far * groups, groups), pl.ds(early, bins - early)],
                      end_send.at[side, far], end_recv.at[far])

    def serve_ends():
        for side, serves, _, _, near, cross_way in sides:
            def serve(side=side, near=near, cross_way=cross_way):
                for far, half, way in ((1, other, cross_way), (0, w, near)):
                    for t in range(owned):
                        j = end_pairs[side, 1, half * owned + t]
                        end_stage[side, far, t] = col[last_chunk][j]
                    end_copy(side, far, way).start()

            pl.when(serves)(serve)

    def ends_done():
        for side, serves, end, _, near, cross_way in sides:
            for far, way in ((1, cross_way), (0, near)):
                copy = end_copy(side, far, way)
                pl.when(serves)(copy.wait_send)
                pl.when(end)(copy.wait_recv)

    def pick_copy(part):
        return remote(PARTNER, stage.at[1, :, :, part], col_pick.at[:, pl.ds(groups, groups), part],
                      pick_sem.at[0], pick_sem.at[1])

    def pick_keep(part):
        return pltpu.make_async_copy(
            stage.at[0, :, :, part], col_pick.at[:, pl.ds(0, groups), part], pick_sem.at[2])

    def pick(c):
        if c == last_chunk:
            relays_sent(True)
            serve_ends()
            pl.when(inner)(lambda: pick_chunk(c))
        else:
            pick_chunk(c)

    def pick_chunk(c):
        k, n = chunks[c]
        for side, half in ((1, other), (0, w)):
            for t in range(owned):
                j = facts[1, half * owned + t]
                stage[side, t, :, k:k + n] = col[c][j]
            (pick_copy if side else pick_keep)(pl.ds(k, n)).start()

    get_facts.wait()
    fill_table(facts, kcol, table, rec.shape[2])
    ahead, both = min(AHEAD, last_chunk), min(BOTH, last_chunk)
    def transform(i):
        fetch(i).wait()
        first, c, n = pieces[i]
        for v in range(first, first + FETCH):
            s = lax.dot_general(table[...], rec[v, c:c + n], (((1,), (1,)), ((), ())),
                                preferred_element_type=jnp.float32)
            scale = 1.0 / jnp.sqrt(jnp.mean(s * s, axis=0, keepdims=True) + 1e-06)
            s = s * scale
            for lane in range(c // 128, (c + n) // 128):
                part = s[:, lane * 128 - c:(lane + 1) * 128 - c]
                spec[lane, pl.ds(v % GROUP, bins, stride=2 * GROUP), :] = part[:bins]
                spec[lane, pl.ds(v % GROUP + GROUP, bins, stride=2 * GROUP), :] = part[bins:]

    def settle(g, lane):
        part = spec[lane].astype(jnp.bfloat16).reshape(bins, 2 * GROUP, 128)
        own[g, :, :, lane * 128:(lane + 1) * 128] = part
        for c, (k, n) in enumerate(chunks):
            col[c][r, g, :, :, lane * 128:(lane + 1) * 128] = part[k:k + n]

    for g in range(groups):
        mine = [i for i, piece in enumerate(pieces) if piece[0] // GROUP == g]
        if g == 0:
            for lane in range(halves):
                for i in mine[lane * len(mine) // halves:(lane + 1) * len(mine) // halves]:
                    transform(i)
                settle(g, lane)
                if lane == 0:
                    pl.semaphore_wait(barrier, 2 + ends)
                for c in range(ahead):
                    send_half(c, lane)
            send_facts()
        else:
            for i in mine:
                transform(i)
            for lane in range(halves):
                settle(g, lane)
        for c in range(2):
            send_own(c, g, False)
            if g > 0:
                send_own(c, g, True)
        to_partner(g).start()
        for way in (RIGHT, LEFT, SIBLING):
            start(way, row_copy(way, own.at[g], q, g))
        for c in range(2, both if g > 0 else 2):
            send_own(c, g, True)
    keep = pltpu.make_async_copy(own, row_set.at[q, pl.ds(0, groups)], local_sem.at[0])
    keep.start()

    last = len(chunks) + rows - 2
    row_work = {}
    for g in range(groups):
        row_work[2 + 2 * g] = lambda g=g: from_partner(g)
        row_work[3 + 2 * g] = lambda g=g: along_x(g)
        row_work[3 + 2 * groups + g] = lambda g=g: along_x(groups + g)
    for step in range(max(last, 3 + 3 * groups)):
        c = 2 + step
        if c < len(chunks):
            send_own(c, None, False)
        if both <= c < ahead:
            for g in range(1, groups):
                send_own(c, g, True)
        elif ahead <= c < last_chunk:
            send_own(c, None, True)
        for h in range(1, rows):
            if 0 <= step - h + 1 < len(chunks):
                hop(h, step - h + 1)
        if 0 <= step - rows + 2 < len(chunks):
            pick(step - rows + 2)
        if step == 1:
            take_pairs()
        if step in row_work:
            row_work[step]()

    rows_done()
    hops_done()
    for n, goes in ((bins, inner), (early, jnp.logical_not(inner))):
        def picks_done(n=n):
            pick_copy(pl.ds(0, n)).wait()
            pick_keep(pl.ds(0, n)).wait()

        pl.when(goes)(picks_done)
    ends_done()
    keep.wait()


def gather(records, facts, bins, rows, cols, owned):
    windows, channels, length = records.shape
    groups = windows // GROUP
    chunks = chunk_list(bins)
    count = len(chunks)
    hbm = pl.BlockSpec(memory_space=pl.ANY)
    dma = pltpu.SemaphoreType.DMA
    tile = (2 * GROUP, channels)
    return pl.pallas_call(
        functools.partial(gather_kernel, rows, cols, chunks),
        out_shape=(
            jax.ShapeDtypeStruct((cols, 2 * groups, bins) + tile, jnp.bfloat16),
            jax.ShapeDtypeStruct((owned, 2 * groups, bins) + tile, jnp.bfloat16)),
        in_specs=[hbm, hbm],
        out_specs=(hbm, hbm),
        scratch_shapes=[
            pltpu.SMEM(facts.shape, jnp.int32),
            dma((1,)),
            pltpu.VMEM((bins, 128), jnp.int32),
            pltpu.VMEM((2 * bins, length), jnp.bfloat16),
            pltpu.VMEM(records.shape, jnp.bfloat16),
            pltpu.VMEM((channels // 128, 2 * bins * GROUP, 128), jnp.float32),
            pltpu.VMEM((groups, bins) + tile, jnp.bfloat16),
            pltpu.VMEM((2, owned, groups, bins) + tile, jnp.bfloat16),
            pltpu.VMEM((2, 2, owned, groups, chunks[-1][1]) + tile, jnp.bfloat16),
            pltpu.VMEM((2,) + facts.shape, jnp.int32),
            pltpu.SMEM((2,) + facts.shape, jnp.int32),
            *[pltpu.VMEM((rows, groups, n) + tile, jnp.bfloat16) for _, n in chunks],
            dma((windows // FETCH + (channels // 128 - 1) * GROUP // FETCH,)),
            dma((1,)),
            dma((1,)),
            dma((3, cols)),
            dma((cols // 2, 2 * groups)),
            dma((cols // 2,)),
            dma((2,)),
            dma((2, rows - 1, WINDOW)),
            dma((rows - 1, count)),
            dma((3,)),
            dma((4,)),
            dma((2, 2)),
            dma((2,)),
        ],
        compiler_params=pltpu.CompilerParams(
            collective_id=0, has_side_effects=True, vmem_limit_bytes=40 * 2**20),
        cost_estimate=pl.CostEstimate(
            flops=4 * windows * channels * length * bins,
            bytes_accessed=windows * channels * length * 2, transcendentals=0),
    )(facts, records)


def cross_kernel(owned, facts, row_set, col_pick, out, ring, sem):
    depth, _, step, channels, _ = ring.shape
    groups = row_set.shape[1]
    chunks = out.shape[4] // step
    piece = step // sem.shape[1]

    def copy(n, p):
        return pltpu.make_async_copy(
            ring.at[n % depth, :, pl.ds(p * piece, piece)],
            out.at[0, 0, n // chunks, :, pl.ds((n % chunks) * step + p * piece, piece)],
            sem.at[n % depth, p])

    pieces = range(sem.shape[1])

    def one(n, _):
        slot = n % depth
        position = lax.axis_index("win") * owned + n // chunks
        i = facts[0, position]
        live = position < facts[3, 0]

        @pl.when(n >= depth)
        def _():
            for p in pieces:
                copy(n - depth, p).wait()

        @pl.when(live)
        def _():
            for p in pieces:
                for t in range(p * piece, (p + 1) * piece):
                    k = (n % chunks) * step + t
                    a = row_set[i, :, k].reshape(-1, channels)
                    b = col_pick[n // chunks, :, k].reshape(a.shape)
                    parts = b.astype(jnp.float32).reshape(groups, 2, GROUP, channels)
                    turned = jnp.concatenate([-parts[:, 1:], parts[:, :1]], axis=1)
                    turned = turned.reshape(a.shape).astype(jnp.bfloat16)
                    both = lax.dot_general(
                        a, jnp.concatenate([b, turned], axis=1), (((0,), (0,)), ((), ())),
                        preferred_element_type=jnp.float32)
                    ring[slot, 0, t] = both[:, :channels].astype(jnp.bfloat16)
                    ring[slot, 1, t] = both[:, channels:].astype(jnp.bfloat16)
                copy(n, p).start()

        @pl.when(jnp.logical_not(live))
        def _():
            ring[slot] = jnp.zeros(ring.shape[1:], jnp.bfloat16)
            for p in pieces:
                copy(n, p).start()

        return 0

    total = owned * chunks
    lax.fori_loop(0, total, one, 0)
    for n in range(max(total - depth, 0), total):
        for p in pieces:
            copy(n, p).wait()


def cross(row_set, col_pick, facts):
    owned, groups, bins, entries, channels = col_pick.shape
    step = math.gcd(bins, 16)
    piece = math.gcd(step, 4)
    smem = pl.BlockSpec(memory_space=pltpu.SMEM)
    vmem = pl.BlockSpec(memory_space=pltpu.VMEM)
    return pl.pallas_call(
        functools.partial(cross_kernel, owned),
        out_shape=jax.ShapeDtypeStruct(
            (1, 1, owned, 2, bins, channels, channels), jnp.bfloat16),
        in_specs=[smem, vmem, vmem],
        out_specs=pl.BlockSpec(memory_space=pl.ANY),
        scratch_shapes=[
            pltpu.VMEM((2, 2, step, channels, channels), jnp.bfloat16),
            pltpu.SemaphoreType.DMA((2, step // piece)),
        ],
        compiler_params=pltpu.CompilerParams(vmem_limit_bytes=40 * 2**20),
        cost_estimate=pl.CostEstimate(
            flops=4 * owned * bins * channels * channels * groups * entries,
            bytes_accessed=4 * owned * bins * channels * channels, transcendentals=0),
    )(facts, row_set, col_pick)


def body(records, tile_pairs, tile_count, bin_index):
    rows, cols = lax.axis_size("row"), lax.axis_size("col")
    owned = tile_pairs.shape[2] // lax.axis_size("win")
    slots, bins = tile_pairs.shape[2], bin_index.shape[0]
    facts = (jnp.pad(jnp.swapaxes(tile_pairs, 2, 3).reshape(2, slots), ((0, 2), (0, 128 - slots)))
             + jnp.pad(bin_index.reshape(1, bins), ((2, 1), (0, 128 - bins)))
             + jnp.pad(tile_count.reshape(1, 1), ((3, 0), (0, 127))))
    row_set, col_pick = gather(records, facts, bins, rows, cols, owned)
    return cross(row_set, col_pick, facts)


def solution(mesh):
    return jax.shard_map(
        body,
        mesh=mesh,
        in_specs=(
            P("win", ("row", "col"), None),
            P("row", "col", None, None),
            P("row", "col"),
            P(),
        ),
        out_specs=P("row", "col", "win", None, None, None, None),
        check_vma=False,
    )
```

```python
import functools
import math

import jax
import jax.numpy as jnp
from jax import lax
from jax.experimental import pallas as pl
from jax.experimental.pallas import tpu as pltpu
from jax.sharding import PartitionSpec as P

GROUP = 8
FETCH = 4
AHEAD = 6
BOTH = 3
WINDOW = 2
UP, DOWN, PARTNER, RIGHT, LEFT, SIBLING, CROSS_UP, CROSS_DOWN = range(8)


def chunk_list(bins):
    size = max(bins // 8, 1)
    starts = list(range(0, 6 * size, size))
    if size > 3:
        starts += [6 * size - size // 2, 6 * size + size // 4]
    return [(a, b - a) for a, b in zip(starts, starts[1:] + [bins])]


def cos_sin(phase, length):
    shift = length.bit_length() - 3
    turn = (phase + (1 << shift >> 1)) >> shift
    x = (phase - (turn << shift)).astype(jnp.float32) * (2.0 * math.pi / length)
    y = x * x
    c = 1.0 + y * (-0.5 + y * (1.0 / 24 + y * (-1.0 / 720 + y * (1.0 / 40320))))
    s = x * (1.0 + y * (-1.0 / 6 + y * (1.0 / 120 + y * (-1.0 / 5040 + y * (1.0 / 362880)))))
    odd = (turn & 1) == 1
    cosine, sine = jnp.where(odd, s, c), jnp.where(odd, c, s)
    cosine = jnp.where(((turn + 1) & 2) == 2, -cosine, cosine)
    sine = jnp.where((turn & 2) == 2, -sine, sine)
    return cosine, sine


def fill_table(facts, kcol, table, length):
    assert length & (length - 1) == 0
    bins = kcol.shape[0]
    for k in range(bins):
        kcol[k:k + 1, :] = jnp.full((1, 128), facts[2, k], jnp.int32)
    for lane in range(0, length, 128):
        samples = lax.broadcasted_iota(jnp.int32, (8, 128), 1) + lane
        taper = 0.5 - 0.5 * cos_sin(samples, length)[0]
        taper = jnp.concatenate([taper] * (bins // 8), axis=0)
        samples = jnp.concatenate([samples] * (bins // 8), axis=0)
        cosine, sine = cos_sin(kcol[...] * samples & (length - 1), length)
        table[:bins, lane:lane + 128] = (taper * cosine).astype(jnp.bfloat16)
        table[bins:, lane:lane + 128] = (-taper * sine).astype(jnp.bfloat16)


def gather_kernel(rows, cols, chunks, facts_hbm, rec_hbm, row_set, col_pick,
                  facts, facts_sem, kcol, table, rec, spec, own, stage,
                  end_stage, end_arrived, end_pairs, *rest):
    col = rest[:len(chunks)]
    (rec_sem, local_sem, partner_send, row_send, row_recv, sibling_recv, hop_send, relay_send, hop_recv,
     pick_sem, pair_sem, end_send, end_recv) = rest[len(chunks):]
    groups, bins = own.shape[0], own.shape[1]
    owned = stage.shape[1]
    w, r, q = lax.axis_index("win"), lax.axis_index("row"), lax.axis_index("col")
    chips = cols // 2
    x = q // 2
    other = 1 - w
    device = {
        UP: (w, r + 1, q), DOWN: (w, r - 1, q), PARTNER: (other, r, q),
        RIGHT: (w, r, q + 2), LEFT: (w, r, q - 2), SIBLING: (w, r, q + 1 - 2 * (q % 2)),
        CROSS_UP: (other, r + 1, q), CROSS_DOWN: (other, r - 1, q),
    }
    exists = {
        UP: r < rows - 1, DOWN: r > 0, PARTNER: None,
        RIGHT: x < chips - 1, LEFT: x > 0, SIBLING: None,
        CROSS_UP: (r == 0) | (r == rows - 2), CROSS_DOWN: (r == 1) | (r == rows - 1),
    }

    last_chunk = len(chunks) - 1
    early = chunks[last_chunk][0]
    inner = (r > 0) & (r < rows - 1)
    to_end = {UP: r == rows - 2, DOWN: r == 1}

    halves = spec.shape[0]
    pieces = [(v, lane * 128, 128) for lane in range(halves) for v in range(0, GROUP, FETCH)]
    pieces += [(v, 0, halves * 128) for v in range(GROUP, groups * GROUP, FETCH)]

    def fetch(i):
        v, c, n = pieces[i]
        part = (pl.ds(v, FETCH), pl.ds(c, n))
        return pltpu.make_async_copy(rec_hbm.at[part], rec.at[part], rec_sem.at[i])

    get_facts = pltpu.make_async_copy(facts_hbm, facts, facts_sem.at[0])
    get_facts.start()
    for i in range(len(pieces)):
        fetch(i).start()

    def guarded(way, f):
        if exists[way] is None:
            f()
        else:
            pl.when(exists[way])(f)

    barrier = pltpu.get_barrier_semaphore()
    for way in range(8):
        guarded(way, lambda way=way: pl.semaphore_signal(
            barrier, inc=1, device_id=device[way], device_id_type=pl.DeviceIdType.MESH))
    ends = sum(exists[way].astype(jnp.int32)
               for way in (UP, DOWN, RIGHT, LEFT, CROSS_UP, CROSS_DOWN))

    def remote(way, src, dst, send_sem, recv_sem):
        return pltpu.make_async_remote_copy(
            src_ref=src, dst_ref=dst, send_sem=send_sem, recv_sem=recv_sem,
            device_id=device[way], device_id_type=pl.DeviceIdType.MESH)

    def start(way, copy):
        guarded(way, copy.start)

    def row_copy(way, src, slot, part):
        recv = sibling_recv.at[slot // 2] if way == SIBLING else row_recv.at[slot // 2, part]
        return remote(way, src, row_set.at[slot, part], row_send.at[way - RIGHT, slot // 2], recv)

    def row_arrived(slot, part):
        row_copy(RIGHT, row_set.at[slot, part], slot, part).wait_recv()

    def row_relay(cond, slot, part, ways):
        def go():
            row_arrived(slot, part)
            for way in ways:
                start(way, row_copy(way, row_set.at[slot, part], slot, part))

        pl.when(cond)(go)

    def along_x(part):
        for d in range(1, chips):
            row_relay(x - d >= 0, q - 2 * d, part, (RIGHT, SIBLING))
            row_relay(x + d < chips, q + 2 * d, part, (LEFT, SIBLING))

    def to_partner(g):
        return remote(PARTNER, own.at[g], row_set.at[q, groups + g],
                      partner_send.at[0], row_recv.at[q // 2, groups + g])

    def from_partner(g):
        part = groups + g
        row_arrived(q, part)
        for way in (RIGHT, LEFT, SIBLING):
            start(way, row_copy(way, row_set.at[q, part], q, part))

    def rows_done():
        def slot_bytes(way, slot):
            return remote(way, row_set.at[slot], row_set.at[slot],
                          row_send.at[way - RIGHT, slot // 2], sibling_recv.at[slot // 2])

        remote(PARTNER, own, own, partner_send.at[0], partner_send.at[0]).wait_send()
        for way in (RIGHT, LEFT, SIBLING):
            guarded(way, slot_bytes(way, q).wait_send)
        for d in range(1, chips):
            for cond, slot, way in ((x - d >= 0, q - 2 * d, RIGHT), (x + d < chips, q + 2 * d, LEFT)):
                def done(slot=slot, way=way):
                    guarded(way, slot_bytes(way, slot).wait_send)
                    slot_bytes(SIBLING, slot).wait_send()

                pl.when(cond)(done)
        for c in range(chips):
            slot_bytes(SIBLING, 2 * c + 1 - q % 2).wait_recv()

    def hop_copy(way, slot, c, src, dst, sem):
        return remote(way, src, dst, sem, hop_recv.at[slot - (1 if way == DOWN else 0), c])

    def start_hop(way, c, copy, wait=False):
        goes = exists[way]
        if c == last_chunk:
            goes = goes & jnp.logical_not(to_end[way])
        pl.when(goes)(copy.wait_send if wait else copy.start)

    def send_own(c, g, to_ends):
        k, n = chunks[c]
        for way in (UP, DOWN):
            goes = to_end[way] if to_ends else exists[way] & jnp.logical_not(to_end[way])
            if g is None:
                copy = hop_copy(way, r, c, own.at[:, pl.ds(k, n)], col[c].at[r], hop_send.at[way])
            else:
                copy = hop_copy(way, r, c, own.at[g, pl.ds(k, n)], col[c].at[r, g],
                                hop_send.at[way])
            pl.when(goes)(copy.start)

    def send_half(c, lane):
        part = (0, pl.ds(*chunks[c]), slice(None), pl.ds(lane * 128, 128))
        for way in (UP, DOWN):
            pl.when(to_end[way])(hop_copy(
                way, r, c, own.at[part], col[c].at[(r, 0) + (slice(None),) * 2 + part[3:]],
                hop_send.at[way]).start)

    def relay(h, way, slot, c):
        return hop_copy(way, slot, c, col[c].at[slot], col[c].at[slot],
                        relay_send.at[way, min(h, max(rows - 2, 1)) - 1, c % WINDOW])

    def ways(h):
        return (r - h >= 0, r - h, UP), (r + h < rows, r + h, DOWN)

    def hop(h, c):
        for cond, slot, way in ways(h):
            def go(slot=slot, way=way):
                relay(h, way, slot, c).wait_recv()
                if c >= WINDOW:
                    start_hop(way, c, relay(h, way, slot, c - WINDOW), True)
                start_hop(way, c, relay(h, way, slot, c))

            pl.when(cond & inner if c == last_chunk else cond)(go)

    def relays_sent(to_ends):
        for h in range(1, rows):
            for cond, slot, way in ways(h):
                goes = to_end[way] if to_ends else exists[way] & jnp.logical_not(to_end[way])
                top = last_chunk if to_ends else len(chunks)
                for c in range(max(top - WINDOW, 0), top):
                    pl.when(cond & goes)(relay(h, way, slot, c).wait_send)

    def hops_done():
        relays_sent(False)
        for way in (UP, DOWN):
            for end, part in ((False, own), (True, own.at[:, pl.ds(0, early)])):
                goes = to_end[way] if end else exists[way] & jnp.logical_not(to_end[way])
                pl.when(goes)(remote(way, part, part, hop_send.at[way], hop_send.at[way]).wait_send)

    sides = ((0, r == 1, r == 0, UP, DOWN, CROSS_DOWN),
             (1, r == rows - 2, r == rows - 1, DOWN, UP, CROSS_UP))

    def pair_copy(side, way):
        return remote(way, facts_hbm, end_arrived.at[side], pair_sem.at[0], pair_sem.at[1 + side])

    def send_facts():
        for side, _, end, way, _, _ in sides:
            pl.when(end)(pair_copy(side, way).start)

    def take_pairs():
        for side, serves, end, way, _, _ in sides:
            def take(side=side, way=way):
                pair_copy(side, way).wait_recv()
                keep = pltpu.make_async_copy(end_arrived.at[side], end_pairs.at[side], pair_sem.at[3])
                keep.start()
                keep.wait()

            pl.when(end)(pair_copy(side, way).wait_send)
            pl.when(serves)(take)

    def end_copy(side, far, way):
        return remote(way, end_stage.at[side, far],
                      col_pick.at[:, pl.ds(far * groups, groups), pl.ds(early, bins - early)],
                      end_send.at[side, far], end_recv.at[far])

    def serve_ends():
        for side, serves, _, _, near, cross_way in sides:
            def serve(side=side, near=near, cross_way=cross_way):
                for far, half, way in ((1, other, cross_way), (0, w, near)):
                    for t in range(owned):
                        j = end_pairs[side, 1, half * owned + t]
                        end_stage[side, far, t] = col[last_chunk][j]
                    end_copy(side, far, way).start()

            pl.when(serves)(serve)

    def ends_done():
        for side, serves, end, _, near, cross_way in sides:
            for far, way in ((1, cross_way), (0, near)):
                copy = end_copy(side, far, way)
                pl.when(serves)(copy.wait_send)
                pl.when(end)(copy.wait_recv)

    def pick_copy(part):
        return remote(PARTNER, stage.at[1, :, :, part], col_pick.at[:, pl.ds(groups, groups), part],
                      pick_sem.at[0], pick_sem.at[1])

    def pick_keep(part):
        return pltpu.make_async_copy(
            stage.at[0, :, :, part], col_pick.at[:, pl.ds(0, groups), part], pick_sem.at[2])

    def pick(c):
        if c == last_chunk:
            relays_sent(True)
            serve_ends()
            pl.when(inner)(lambda: pick_chunk(c))
        else:
            pick_chunk(c)

    def pick_chunk(c):
        k, n = chunks[c]
        for side, half in ((1, other), (0, w)):
            for t in range(owned):
                j = facts[1, half * owned + t]
                stage[side, t, :, k:k + n] = col[c][j]
            (pick_copy if side else pick_keep)(pl.ds(k, n)).start()

    get_facts.wait()
    fill_table(facts, kcol, table, rec.shape[2])
    ahead, both = min(AHEAD, last_chunk), min(BOTH, last_chunk)
    def transform(i):
        fetch(i).wait()
        first, c, n = pieces[i]
        for v in range(first, first + FETCH):
            s = lax.dot_general(table[...], rec[v, c:c + n], (((1,), (1,)), ((), ())),
                                preferred_element_type=jnp.float32)
            scale = 1.0 / jnp.sqrt(jnp.mean(s * s, axis=0, keepdims=True) + 1e-06)
            s = s * scale
            for lane in range(c // 128, (c + n) // 128):
                part = s[:, lane * 128 - c:(lane + 1) * 128 - c]
                spec[lane, pl.ds(v % GROUP, bins, stride=2 * GROUP), :] = part[:bins]
                spec[lane, pl.ds(v % GROUP + GROUP, bins, stride=2 * GROUP), :] = part[bins:]

    def settle(g, lane):
        part = spec[lane].astype(jnp.bfloat16).reshape(bins, 2 * GROUP, 128)
        own[g, :, :, lane * 128:(lane + 1) * 128] = part
        for c, (k, n) in enumerate(chunks):
            col[c][r, g, :, :, lane * 128:(lane + 1) * 128] = part[k:k + n]

    for g in range(groups):
        mine = [i for i, piece in enumerate(pieces) if piece[0] // GROUP == g]
        if g == 0:
            for lane in range(halves):
                for i in mine[lane * len(mine) // halves:(lane + 1) * len(mine) // halves]:
                    transform(i)
                settle(g, lane)
                if lane == 0:
                    pl.semaphore_wait(barrier, 2 + ends)
                for c in range(ahead):
                    send_half(c, lane)
            send_facts()
        else:
            for i in mine:
                transform(i)
            for lane in range(halves):
                settle(g, lane)
        for c in range(2):
            send_own(c, g, False)
            if g > 0:
                send_own(c, g, True)
        to_partner(g).start()
        for way in (RIGHT, LEFT, SIBLING):
            start(way, row_copy(way, own.at[g], q, g))
        for c in range(2, both if g > 0 else 2):
            send_own(c, g, True)
    keep = pltpu.make_async_copy(own, row_set.at[q, pl.ds(0, groups)], local_sem.at[0])
    keep.start()

    last = len(chunks) + rows - 2
    row_work = {}
    for g in range(groups):
        row_work[2 + 2 * g] = lambda g=g: from_partner(g)
        row_work[3 + 2 * g] = lambda g=g: along_x(g)
        row_work[3 + 2 * groups + g] = lambda g=g: along_x(groups + g)
    for step in range(max(last, 3 + 3 * groups)):
        c = 2 + step
        if c < len(chunks):
            send_own(c, None, False)
        if both <= c < ahead:
            for g in range(1, groups):
                send_own(c, g, True)
        elif ahead <= c < last_chunk:
            send_own(c, None, True)
        for h in range(1, rows):
            if 0 <= step - h + 1 < len(chunks):
                hop(h, step - h + 1)
        if 0 <= step - rows + 2 < len(chunks):
            pick(step - rows + 2)
        if step == 1:
            take_pairs()
        if step in row_work:
            row_work[step]()

    rows_done()
    hops_done()
    for n, goes in ((bins, inner), (early, jnp.logical_not(inner))):
        def picks_done(n=n):
            pick_copy(pl.ds(0, n)).wait()
            pick_keep(pl.ds(0, n)).wait()

        pl.when(goes)(picks_done)
    ends_done()
    keep.wait()


def gather(records, facts, bins, rows, cols, owned):
    windows, channels, length = records.shape
    groups = windows // GROUP
    chunks = chunk_list(bins)
    count = len(chunks)
    hbm = pl.BlockSpec(memory_space=pl.ANY)
    dma = pltpu.SemaphoreType.DMA
    tile = (2 * GROUP, channels)
    return pl.pallas_call(
        functools.partial(gather_kernel, rows, cols, chunks),
        out_shape=(
            jax.ShapeDtypeStruct((cols, 2 * groups, bins) + tile, jnp.bfloat16),
            jax.ShapeDtypeStruct((owned, 2 * groups, bins) + tile, jnp.bfloat16)),
        in_specs=[hbm, hbm],
        out_specs=(hbm, hbm),
        scratch_shapes=[
            pltpu.SMEM(facts.shape, jnp.int32),
            dma((1,)),
            pltpu.VMEM((bins, 128), jnp.int32),
            pltpu.VMEM((2 * bins, length), jnp.bfloat16),
            pltpu.VMEM(records.shape, jnp.bfloat16),
            pltpu.VMEM((channels // 128, 2 * bins * GROUP, 128), jnp.float32),
            pltpu.VMEM((groups, bins) + tile, jnp.bfloat16),
            pltpu.VMEM((2, owned, groups, bins) + tile, jnp.bfloat16),
            pltpu.VMEM((2, 2, owned, groups, chunks[-1][1]) + tile, jnp.bfloat16),
            pltpu.VMEM((2,) + facts.shape, jnp.int32),
            pltpu.SMEM((2,) + facts.shape, jnp.int32),
            *[pltpu.VMEM((rows, groups, n) + tile, jnp.bfloat16) for _, n in chunks],
            dma((windows // FETCH + (channels // 128 - 1) * GROUP // FETCH,)),
            dma((1,)),
            dma((1,)),
            dma((3, cols // 2)),
            dma((cols // 2, 2 * groups)),
            dma((cols // 2,)),
            dma((2,)),
            dma((2, max(rows - 2, 1), WINDOW)),
            dma((rows - 1, count)),
            dma((3,)),
            dma((4,)),
            dma((2, 2)),
            dma((2,)),
        ],
        compiler_params=pltpu.CompilerParams(
            collective_id=0, has_side_effects=True, vmem_limit_bytes=40 * 2**20),
        cost_estimate=pl.CostEstimate(
            flops=4 * windows * channels * length * bins,
            bytes_accessed=windows * channels * length * 2, transcendentals=0),
    )(facts, records)


def cross_kernel(owned, facts, row_set, col_pick, out, ring, sem):
    depth, _, step, channels, _ = ring.shape
    groups = row_set.shape[1]
    chunks = out.shape[4] // step
    piece = step // sem.shape[1]

    def copy(n, p):
        return pltpu.make_async_copy(
            ring.at[n % depth, :, pl.ds(p * piece, piece)],
            out.at[0, 0, n // chunks, :, pl.ds((n % chunks) * step + p * piece, piece)],
            sem.at[n % depth, p])

    pieces = range(sem.shape[1])

    def one(n, _):
        slot = n % depth
        position = lax.axis_index("win") * owned + n // chunks
        i = facts[0, position]
        live = position < facts[3, 0]

        @pl.when(n >= depth)
        def _():
            for p in pieces:
                copy(n - depth, p).wait()

        @pl.when(live)
        def _():
            for p in pieces:
                for t in range(p * piece, (p + 1) * piece):
                    k = (n % chunks) * step + t
                    a = row_set[i, :, k].reshape(-1, channels)
                    b = col_pick[n // chunks, :, k].reshape(a.shape)
                    parts = b.astype(jnp.float32).reshape(groups, 2, GROUP, channels)
                    turned = jnp.concatenate([-parts[:, 1:], parts[:, :1]], axis=1)
                    turned = turned.reshape(a.shape).astype(jnp.bfloat16)
                    both = lax.dot_general(
                        a, jnp.concatenate([b, turned], axis=1), (((0,), (0,)), ((), ())),
                        preferred_element_type=jnp.float32)
                    ring[slot, 0, t] = both[:, :channels].astype(jnp.bfloat16)
                    ring[slot, 1, t] = both[:, channels:].astype(jnp.bfloat16)
                copy(n, p).start()

        @pl.when(jnp.logical_not(live))
        def _():
            ring[slot] = jnp.zeros(ring.shape[1:], jnp.bfloat16)
            for p in pieces:
                copy(n, p).start()

        return 0

    total = owned * chunks
    lax.fori_loop(0, total, one, 0)
    for n in range(max(total - depth, 0), total):
        for p in pieces:
            copy(n, p).wait()


def cross(row_set, col_pick, facts):
    owned, groups, bins, entries, channels = col_pick.shape
    step = math.gcd(bins, 16)
    piece = math.gcd(step, 4)
    smem = pl.BlockSpec(memory_space=pltpu.SMEM)
    vmem = pl.BlockSpec(memory_space=pltpu.VMEM)
    return pl.pallas_call(
        functools.partial(cross_kernel, owned),
        out_shape=jax.ShapeDtypeStruct(
            (1, 1, owned, 2, bins, channels, channels), jnp.bfloat16),
        in_specs=[smem, vmem, vmem],
        out_specs=pl.BlockSpec(memory_space=pl.ANY),
        scratch_shapes=[
            pltpu.VMEM((2, 2, step, channels, channels), jnp.bfloat16),
            pltpu.SemaphoreType.DMA((2, step // piece)),
        ],
        compiler_params=pltpu.CompilerParams(vmem_limit_bytes=40 * 2**20),
        cost_estimate=pl.CostEstimate(
            flops=4 * owned * bins * channels * channels * groups * entries,
            bytes_accessed=4 * owned * bins * channels * channels, transcendentals=0),
    )(facts, row_set, col_pick)


def body(records, tile_pairs, tile_count, bin_index):
    rows, cols = lax.axis_size("row"), lax.axis_size("col")
    owned = tile_pairs.shape[2] // lax.axis_size("win")
    slots, bins = tile_pairs.shape[2], bin_index.shape[0]
    facts = (jnp.pad(jnp.swapaxes(tile_pairs, 2, 3).reshape(2, slots), ((0, 2), (0, 128 - slots)))
             + jnp.pad(bin_index.reshape(1, bins), ((2, 1), (0, 128 - bins)))
             + jnp.pad(tile_count.reshape(1, 1), ((3, 0), (0, 127))))
    row_set, col_pick = gather(records, facts, bins, rows, cols, owned)
    return cross(row_set, col_pick, facts)


def solution(mesh):
    return jax.shard_map(
        body,
        mesh=mesh,
        in_specs=(
            P("win", ("row", "col"), None),
            P("row", "col", None, None),
            P("row", "col"),
            P(),
        ),
        out_specs=P("row", "col", "win", None, None, None, None),
        check_vma=False,
    )
```

```python
import functools
import math

import jax
import jax.numpy as jnp
from jax import lax
from jax.experimental import pallas as pl
from jax.experimental.pallas import tpu as pltpu
from jax.sharding import PartitionSpec as P

GROUP = 8
FETCH = 4
AHEAD = 6
BOTH = 4
WINDOW = 2
UP, DOWN, PARTNER, RIGHT, LEFT, SIBLING, CROSS_UP, CROSS_DOWN = range(8)


def chunk_list(bins):
    size = max(bins // 8, 1)
    starts = list(range(0, 6 * size, size))
    if size > 3:
        starts += [6 * size - size // 2, 6 * size + size // 4]
    return [(a, b - a) for a, b in zip(starts, starts[1:] + [bins])]


def cos_sin(phase, length):
    shift = length.bit_length() - 3
    turn = (phase + (1 << shift >> 1)) >> shift
    x = (phase - (turn << shift)).astype(jnp.float32) * (2.0 * math.pi / length)
    y = x * x
    c = 1.0 + y * (-0.5 + y * (1.0 / 24 + y * (-1.0 / 720 + y * (1.0 / 40320))))
    s = x * (1.0 + y * (-1.0 / 6 + y * (1.0 / 120 + y * (-1.0 / 5040 + y * (1.0 / 362880)))))
    odd = (turn & 1) == 1
    cosine, sine = jnp.where(odd, s, c), jnp.where(odd, c, s)
    cosine = jnp.where(((turn + 1) & 2) == 2, -cosine, cosine)
    sine = jnp.where((turn & 2) == 2, -sine, sine)
    return cosine, sine


def fill_table(facts, kcol, table, length):
    assert length & (length - 1) == 0
    bins = kcol.shape[0]
    for k in range(bins):
        kcol[k:k + 1, :] = jnp.full((1, 128), facts[2, k], jnp.int32)
    for lane in range(0, length, 128):
        samples = lax.broadcasted_iota(jnp.int32, (8, 128), 1) + lane
        taper = 0.5 - 0.5 * cos_sin(samples, length)[0]
        taper = jnp.concatenate([taper] * (bins // 8), axis=0)
        samples = jnp.concatenate([samples] * (bins // 8), axis=0)
        cosine, sine = cos_sin(kcol[...] * samples & (length - 1), length)
        table[:bins, lane:lane + 128] = (taper * cosine).astype(jnp.bfloat16)
        table[bins:, lane:lane + 128] = (-taper * sine).astype(jnp.bfloat16)


def gather_kernel(rows, cols, chunks, facts_hbm, rec_hbm, row_set, col_pick,
                  facts, facts_sem, kcol, table, rec, spec, own, stage,
                  end_stage, end_arrived, end_pairs, *rest):
    col = rest[:len(chunks)]
    (rec_sem, local_sem, partner_send, row_send, row_recv, sibling_recv, hop_send, relay_send, hop_recv,
     pick_sem, pair_sem, end_send, end_recv) = rest[len(chunks):]
    groups, bins = own.shape[0], own.shape[1]
    owned = stage.shape[1]
    w, r, q = lax.axis_index("win"), lax.axis_index("row"), lax.axis_index("col")
    chips = cols // 2
    x = q // 2
    other = 1 - w
    device = {
        UP: (w, r + 1, q), DOWN: (w, r - 1, q), PARTNER: (other, r, q),
        RIGHT: (w, r, q + 2), LEFT: (w, r, q - 2), SIBLING: (w, r, q + 1 - 2 * (q % 2)),
        CROSS_UP: (other, r + 1, q), CROSS_DOWN: (other, r - 1, q),
    }
    exists = {
        UP: r < rows - 1, DOWN: r > 0, PARTNER: None,
        RIGHT: x < chips - 1, LEFT: x > 0, SIBLING: None,
        CROSS_UP: (r == 0) | (r == rows - 2), CROSS_DOWN: (r == 1) | (r == rows - 1),
    }

    last_chunk = len(chunks) - 1
    early = chunks[last_chunk][0]
    inner = (r > 0) & (r < rows - 1)
    to_end = {UP: r == rows - 2, DOWN: r == 1}

    halves = spec.shape[0]
    pieces = [(v, lane * 128, 128) for lane in range(halves) for v in range(0, GROUP, FETCH)]
    pieces += [(v, 0, halves * 128) for v in range(GROUP, groups * GROUP, FETCH)]

    def fetch(i):
        v, c, n = pieces[i]
        part = (pl.ds(v, FETCH), pl.ds(c, n))
        return pltpu.make_async_copy(rec_hbm.at[part], rec.at[part], rec_sem.at[i])

    get_facts = pltpu.make_async_copy(facts_hbm, facts, facts_sem.at[0])
    get_facts.start()
    for i in range(len(pieces)):
        fetch(i).start()

    def guarded(way, f):
        if exists[way] is None:
            f()
        else:
            pl.when(exists[way])(f)

    barrier = pltpu.get_barrier_semaphore()
    for way in range(8):
        guarded(way, lambda way=way: pl.semaphore_signal(
            barrier, inc=1, device_id=device[way], device_id_type=pl.DeviceIdType.MESH))
    ends = sum(exists[way].astype(jnp.int32)
               for way in (UP, DOWN, RIGHT, LEFT, CROSS_UP, CROSS_DOWN))

    def remote(way, src, dst, send_sem, recv_sem):
        return pltpu.make_async_remote_copy(
            src_ref=src, dst_ref=dst, send_sem=send_sem, recv_sem=recv_sem,
            device_id=device[way], device_id_type=pl.DeviceIdType.MESH)

    def start(way, copy):
        guarded(way, copy.start)

    def row_copy(way, src, slot, part):
        recv = sibling_recv.at[slot // 2] if way == SIBLING else row_recv.at[slot // 2, part]
        return remote(way, src, row_set.at[slot, part], row_send.at[way - RIGHT, slot // 2], recv)

    def row_arrived(slot, part):
        row_copy(RIGHT, row_set.at[slot, part], slot, part).wait_recv()

    def row_relay(cond, slot, part, ways):
        def go():
            row_arrived(slot, part)
            for way in ways:
                start(way, row_copy(way, row_set.at[slot, part], slot, part))

        pl.when(cond)(go)

    def along_x(part):
        for d in range(1, chips):
            row_relay(x - d >= 0, q - 2 * d, part, (RIGHT, SIBLING))
            row_relay(x + d < chips, q + 2 * d, part, (LEFT, SIBLING))

    def to_partner(g):
        return remote(PARTNER, own.at[g], row_set.at[q, groups + g],
                      partner_send.at[0], row_recv.at[q // 2, groups + g])

    def from_partner(g):
        part = groups + g
        row_arrived(q, part)
        for way in (RIGHT, LEFT, SIBLING):
            start(way, row_copy(way, row_set.at[q, part], q, part))

    def rows_done():
        def slot_bytes(way, slot):
            return remote(way, row_set.at[slot], row_set.at[slot],
                          row_send.at[way - RIGHT, slot // 2], sibling_recv.at[slot // 2])

        remote(PARTNER, own, own, partner_send.at[0], partner_send.at[0]).wait_send()
        for way in (RIGHT, LEFT, SIBLING):
            guarded(way, slot_bytes(way, q).wait_send)
        for d in range(1, chips):
            for cond, slot, way in ((x - d >= 0, q - 2 * d, RIGHT), (x + d < chips, q + 2 * d, LEFT)):
                def done(slot=slot, way=way):
                    guarded(way, slot_bytes(way, slot).wait_send)
                    slot_bytes(SIBLING, slot).wait_send()

                pl.when(cond)(done)
        for c in range(chips):
            slot_bytes(SIBLING, 2 * c + 1 - q % 2).wait_recv()

    def hop_copy(way, slot, c, src, dst, sem):
        return remote(way, src, dst, sem, hop_recv.at[slot - (1 if way == DOWN else 0), c])

    def start_hop(way, c, copy, wait=False):
        goes = exists[way]
        if c == last_chunk:
            goes = goes & jnp.logical_not(to_end[way])
        pl.when(goes)(copy.wait_send if wait else copy.start)

    def send_own(c, g, to_ends):
        k, n = chunks[c]
        for way in (UP, DOWN):
            goes = to_end[way] if to_ends else exists[way] & jnp.logical_not(to_end[way])
            if g is None:
                copy = hop_copy(way, r, c, own.at[:, pl.ds(k, n)], col[c].at[r], hop_send.at[way])
            else:
                copy = hop_copy(way, r, c, own.at[g, pl.ds(k, n)], col[c].at[r, g],
                                hop_send.at[way])
            pl.when(goes)(copy.start)

    def send_half(c, lane):
        part = (0, pl.ds(*chunks[c]), slice(None), pl.ds(lane * 128, 128))
        for way in (UP, DOWN):
            pl.when(to_end[way])(hop_copy(
                way, r, c, own.at[part], col[c].at[(r, 0) + (slice(None),) * 2 + part[3:]],
                hop_send.at[way]).start)

    def relay(h, way, slot, c):
        return hop_copy(way, slot, c, col[c].at[slot], col[c].at[slot],
                        relay_send.at[way, min(h, max(rows - 2, 1)) - 1, c % WINDOW])

    def ways(h):
        return (r - h >= 0, r - h, UP), (r + h < rows, r + h, DOWN)

    def hop(h, c):
        for cond, slot, way in ways(h):
            def go(slot=slot, way=way):
                relay(h, way, slot, c).wait_recv()
                if c >= WINDOW:
                    start_hop(way, c, relay(h, way, slot, c - WINDOW), True)
                start_hop(way, c, relay(h, way, slot, c))

            pl.when(cond & inner if c == last_chunk else cond)(go)

    def relays_sent(to_ends):
        for h in range(1, rows):
            for cond, slot, way in ways(h):
                goes = to_end[way] if to_ends else exists[way] & jnp.logical_not(to_end[way])
                top = last_chunk if to_ends else len(chunks)
                for c in range(max(top - WINDOW, 0), top):
                    pl.when(cond & goes)(relay(h, way, slot, c).wait_send)

    def hops_done():
        relays_sent(False)
        for way in (UP, DOWN):
            for end, part in ((False, own), (True, own.at[:, pl.ds(0, early)])):
                goes = to_end[way] if end else exists[way] & jnp.logical_not(to_end[way])
                pl.when(goes)(remote(way, part, part, hop_send.at[way], hop_send.at[way]).wait_send)

    sides = ((0, r == 1, r == 0, UP, DOWN, CROSS_DOWN),
             (1, r == rows - 2, r == rows - 1, DOWN, UP, CROSS_UP))

    def pair_copy(side, way):
        return remote(way, facts_hbm, end_arrived.at[side], pair_sem.at[0], pair_sem.at[1 + side])

    def send_facts():
        for side, _, end, way, _, _ in sides:
            pl.when(end)(pair_copy(side, way).start)

    def take_pairs():
        for side, serves, end, way, _, _ in sides:
            def take(side=side, way=way):
                pair_copy(side, way).wait_recv()
                keep = pltpu.make_async_copy(end_arrived.at[side], end_pairs.at[side], pair_sem.at[3])
                keep.start()
                keep.wait()

            pl.when(end)(pair_copy(side, way).wait_send)
            pl.when(serves)(take)

    def end_copy(side, far, way):
        return remote(way, end_stage.at[side, far],
                      col_pick.at[:, pl.ds(far * groups, groups), pl.ds(early, bins - early)],
                      end_send.at[side, far], end_recv.at[far])

    def serve_ends():
        for side, serves, _, _, near, cross_way in sides:
            def serve(side=side, near=near, cross_way=cross_way):
                for far, half, way in ((1, other, cross_way), (0, w, near)):
                    for t in range(owned):
                        j = end_pairs[side, 1, half * owned + t]
                        end_stage[side, far, t] = col[last_chunk][j]
                    end_copy(side, far, way).start()

            pl.when(serves)(serve)

    def ends_done():
        for side, serves, end, _, near, cross_way in sides:
            for far, way in ((1, cross_way), (0, near)):
                copy = end_copy(side, far, way)
                pl.when(serves)(copy.wait_send)
                pl.when(end)(copy.wait_recv)

    def pick_copy(part):
        return remote(PARTNER, stage.at[1, :, :, part], col_pick.at[:, pl.ds(groups, groups), part],
                      pick_sem.at[0], pick_sem.at[1])

    def pick_keep(part):
        return pltpu.make_async_copy(
            stage.at[0, :, :, part], col_pick.at[:, pl.ds(0, groups), part], pick_sem.at[2])

    def pick(c):
        if c == last_chunk:
            relays_sent(True)
            serve_ends()
            pl.when(inner)(lambda: pick_chunk(c))
        else:
            pick_chunk(c)

    def pick_chunk(c):
        k, n = chunks[c]
        for side, half in ((1, other), (0, w)):
            for t in range(owned):
                j = facts[1, half * owned + t]
                stage[side, t, :, k:k + n] = col[c][j]
            (pick_copy if side else pick_keep)(pl.ds(k, n)).start()

    get_facts.wait()
    fill_table(facts, kcol, table, rec.shape[2])
    ahead, both = min(AHEAD, last_chunk), min(BOTH, last_chunk)
    def transform(i):
        fetch(i).wait()
        first, c, n = pieces[i]
        for v in range(first, first + FETCH):
            s = lax.dot_general(table[...], rec[v, c:c + n], (((1,), (1,)), ((), ())),
                                preferred_element_type=jnp.float32)
            scale = 1.0 / jnp.sqrt(jnp.mean(s * s, axis=0, keepdims=True) + 1e-06)
            s = s * scale
            for lane in range(c // 128, (c + n) // 128):
                part = s[:, lane * 128 - c:(lane + 1) * 128 - c]
                spec[lane, pl.ds(v % GROUP, bins, stride=2 * GROUP), :] = part[:bins]
                spec[lane, pl.ds(v % GROUP + GROUP, bins, stride=2 * GROUP), :] = part[bins:]

    def settle(g, lane):
        part = spec[lane].astype(jnp.bfloat16).reshape(bins, 2 * GROUP, 128)
        own[g, :, :, lane * 128:(lane + 1) * 128] = part
        for c, (k, n) in enumerate(chunks):
            col[c][r, g, :, :, lane * 128:(lane + 1) * 128] = part[k:k + n]

    for g in range(groups):
        mine = [i for i, piece in enumerate(pieces) if piece[0] // GROUP == g]
        if g == 0:
            for lane in range(halves):
                for i in mine[lane * len(mine) // halves:(lane + 1) * len(mine) // halves]:
                    transform(i)
                settle(g, lane)
                if lane == 0:
                    pl.semaphore_wait(barrier, 2 + ends)
                for c in range(ahead):
                    send_half(c, lane)
            send_facts()
        else:
            for i in mine:
                transform(i)
            for lane in range(halves):
                settle(g, lane)
        for c in range(2):
            send_own(c, g, False)
            if g > 0:
                send_own(c, g, True)
        to_partner(g).start()
        for way in (RIGHT, LEFT, SIBLING):
            start(way, row_copy(way, own.at[g], q, g))
        for c in range(2, both if g > 0 else 2):
            send_own(c, g, True)
    keep = pltpu.make_async_copy(own, row_set.at[q, pl.ds(0, groups)], local_sem.at[0])
    keep.start()

    last = len(chunks) + rows - 2
    row_work = {}
    for g in range(groups):
        row_work[2 + 2 * g] = lambda g=g: from_partner(g)
        row_work[3 + 2 * g] = lambda g=g: along_x(g)
        row_work[3 + 2 * groups + g] = lambda g=g: along_x(groups + g)
    for step in range(max(last, 3 + 3 * groups)):
        c = 2 + step
        if c < len(chunks):
            send_own(c, None, False)
        if both <= c < ahead:
            for g in range(1, groups):
                send_own(c, g, True)
        elif ahead <= c < last_chunk:
            send_own(c, None, True)
        for h in range(1, rows):
            if 0 <= step - h + 1 < len(chunks):
                hop(h, step - h + 1)
        if 0 <= step - rows + 2 < len(chunks):
            pick(step - rows + 2)
        if step == 1:
            take_pairs()
        if step in row_work:
            row_work[step]()

    rows_done()
    hops_done()
    for n, goes in ((bins, inner), (early, jnp.logical_not(inner))):
        def picks_done(n=n):
            pick_copy(pl.ds(0, n)).wait()
            pick_keep(pl.ds(0, n)).wait()

        pl.when(goes)(picks_done)
    ends_done()
    keep.wait()


def gather(records, facts, bins, rows, cols, owned):
    windows, channels, length = records.shape
    groups = windows // GROUP
    chunks = chunk_list(bins)
    count = len(chunks)
    hbm = pl.BlockSpec(memory_space=pl.ANY)
    dma = pltpu.SemaphoreType.DMA
    tile = (2 * GROUP, channels)
    return pl.pallas_call(
        functools.partial(gather_kernel, rows, cols, chunks),
        out_shape=(
            jax.ShapeDtypeStruct((cols, 2 * groups, bins) + tile, jnp.bfloat16),
            jax.ShapeDtypeStruct((owned, 2 * groups, bins) + tile, jnp.bfloat16)),
        in_specs=[hbm, hbm],
        out_specs=(hbm, hbm),
        scratch_shapes=[
            pltpu.SMEM(facts.shape, jnp.int32),
            dma((1,)),
            pltpu.VMEM((bins, 128), jnp.int32),
            pltpu.VMEM((2 * bins, length), jnp.bfloat16),
            pltpu.VMEM(records.shape, jnp.bfloat16),
            pltpu.VMEM((channels // 128, 2 * bins * GROUP, 128), jnp.float32),
            pltpu.VMEM((groups, bins) + tile, jnp.bfloat16),
            pltpu.VMEM((2, owned, groups, bins) + tile, jnp.bfloat16),
            pltpu.VMEM((2, 2, owned, groups, chunks[-1][1]) + tile, jnp.bfloat16),
            pltpu.VMEM((2,) + facts.shape, jnp.int32),
            pltpu.SMEM((2,) + facts.shape, jnp.int32),
            *[pltpu.VMEM((rows, groups, n) + tile, jnp.bfloat16) for _, n in chunks],
            dma((windows // FETCH + (channels // 128 - 1) * GROUP // FETCH,)),
            dma((1,)),
            dma((1,)),
            dma((3, cols // 2)),
            dma((cols // 2, 2 * groups)),
            dma((cols // 2,)),
            dma((2,)),
            dma((2, max(rows - 2, 1), WINDOW)),
            dma((rows - 1, count)),
            dma((3,)),
            dma((4,)),
            dma((2, 2)),
            dma((2,)),
        ],
        compiler_params=pltpu.CompilerParams(
            collective_id=0, has_side_effects=True, vmem_limit_bytes=40 * 2**20),
        cost_estimate=pl.CostEstimate(
            flops=4 * windows * channels * length * bins,
            bytes_accessed=windows * channels * length * 2, transcendentals=0),
    )(facts, records)


def cross_kernel(owned, facts, row_set, col_pick, out, ring, sem):
    depth, _, step, channels, _ = ring.shape
    groups = row_set.shape[1]
    chunks = out.shape[4] // step
    piece = step // sem.shape[1]

    def copy(n, p):
        return pltpu.make_async_copy(
            ring.at[n % depth, :, pl.ds(p * piece, piece)],
            out.at[0, 0, n // chunks, :, pl.ds((n % chunks) * step + p * piece, piece)],
            sem.at[n % depth, p])

    pieces = range(sem.shape[1])

    def one(n, _):
        slot = n % depth
        position = lax.axis_index("win") * owned + n // chunks
        i = facts[0, position]
        live = position < facts[3, 0]

        @pl.when(n >= depth)
        def _():
            for p in pieces:
                copy(n - depth, p).wait()

        @pl.when(live)
        def _():
            for p in pieces:
                for t in range(p * piece, (p + 1) * piece):
                    k = (n % chunks) * step + t
                    a = row_set[i, :, k].reshape(-1, channels)
                    b = col_pick[n // chunks, :, k].reshape(a.shape)
                    parts = b.astype(jnp.float32).reshape(groups, 2, GROUP, channels)
                    turned = jnp.concatenate([-parts[:, 1:], parts[:, :1]], axis=1)
                    turned = turned.reshape(a.shape).astype(jnp.bfloat16)
                    both = lax.dot_general(
                        a, jnp.concatenate([b, turned], axis=1), (((0,), (0,)), ((), ())),
                        preferred_element_type=jnp.float32)
                    ring[slot, 0, t] = both[:, :channels].astype(jnp.bfloat16)
                    ring[slot, 1, t] = both[:, channels:].astype(jnp.bfloat16)
                copy(n, p).start()

        @pl.when(jnp.logical_not(live))
        def _():
            ring[slot] = jnp.zeros(ring.shape[1:], jnp.bfloat16)
            for p in pieces:
                copy(n, p).start()

        return 0

    total = owned * chunks
    lax.fori_loop(0, total, one, 0)
    for n in range(max(total - depth, 0), total):
        for p in pieces:
            copy(n, p).wait()


def cross(row_set, col_pick, facts):
    owned, groups, bins, entries, channels = col_pick.shape
    step = math.gcd(bins, 16)
    piece = math.gcd(step, 4)
    smem = pl.BlockSpec(memory_space=pltpu.SMEM)
    vmem = pl.BlockSpec(memory_space=pltpu.VMEM)
    return pl.pallas_call(
        functools.partial(cross_kernel, owned),
        out_shape=jax.ShapeDtypeStruct(
            (1, 1, owned, 2, bins, channels, channels), jnp.bfloat16),
        in_specs=[smem, vmem, vmem],
        out_specs=pl.BlockSpec(memory_space=pl.ANY),
        scratch_shapes=[
            pltpu.VMEM((2, 2, step, channels, channels), jnp.bfloat16),
            pltpu.SemaphoreType.DMA((2, step // piece)),
        ],
        compiler_params=pltpu.CompilerParams(vmem_limit_bytes=40 * 2**20),
        cost_estimate=pl.CostEstimate(
            flops=4 * owned * bins * channels * channels * groups * entries,
            bytes_accessed=4 * owned * bins * channels * channels, transcendentals=0),
    )(facts, row_set, col_pick)


def body(records, tile_pairs, tile_count, bin_index):
    rows, cols = lax.axis_size("row"), lax.axis_size("col")
    owned = tile_pairs.shape[2] // lax.axis_size("win")
    slots, bins = tile_pairs.shape[2], bin_index.shape[0]
    facts = (jnp.pad(jnp.swapaxes(tile_pairs, 2, 3).reshape(2, slots), ((0, 2), (0, 128 - slots)))
             + jnp.pad(bin_index.reshape(1, bins), ((2, 1), (0, 128 - bins)))
             + jnp.pad(tile_count.reshape(1, 1), ((3, 0), (0, 127))))
    row_set, col_pick = gather(records, facts, bins, rows, cols, owned)
    return cross(row_set, col_pick, facts)


def solution(mesh):
    return jax.shard_map(
        body,
        mesh=mesh,
        in_specs=(
            P("win", ("row", "col"), None),
            P("row", "col", None, None),
            P("row", "col"),
            P(),
        ),
        out_specs=P("row", "col", "win", None, None, None, None),
        check_vma=False,
    )
```
